256 devices in a mesh: blk: 16 (over x, z_hi, core), grp: 16 (over z_lo, y).
Axes of the slice: x: 4, y: 4, z: 8 (z_hi: 2, z_lo: 4; z = z_hi * 4 + z_lo), core: 2. Of those that a mesh axis runs over, the one named last changes fastest.
Arguments:
- img_feat: bfloat16 [49152, 768], P(('blk', 'grp')), may hold values from -6 to 6
- txt_feat: bfloat16 [49152, 768], P(('blk', 'grp')), may hold values from -6 to 6
- img_head: bfloat16 [768, 768], replicated, may hold values from -0.21875 to 0.21875
- txt_head: bfloat16 [768, 768], replicated, may hold values from -0.21875 to 0.21875
- logit_scale: float32 [1], replicated, may hold values from 5 to 15
- logit_bias: float32 [1], replicated, may hold values from -8 to -4
- pair_offset: int32 [49152], P(('blk', 'grp')), may hold values from 0 to 1
Outputs:
- img_feat_grad: float32 [49152, 768], P(('blk', 'grp'))
- txt_feat_grad: float32 [49152, 768], P(('blk', 'grp'))
- img_head_grad: float32 [768, 768], replicated
- txt_head_grad: float32 [768, 768], replicated
- mean_loss: float32 [1], replicated
The draws below stay inside these ranges and needn't reach their ends.
Inputs may be any that keep to these rules, and one draw needn't show every extreme that they name: `pair_offset`: each image's caption lies in one of the 2 text blocks that it is scored against.
All inputs are finite; a program needn't handle non-finite values.
Results may differ from the reference program's by a relative error of at most 0.0047.
Values may be sent and summed in bfloat16 or wider, within the bound.
No kernel may reach another device: no remote copies, remote signals or barrier semaphores. Data moves between devices by JAX's collectives and lax.ppermute only.
A program may use at most 192 MiB of HBM per device.

```python
import math
import jax
import jax.numpy as jnp
from jax import lax

E = 768
D = 768
ROWS = 192
STEPS = 2
NIMG = 49152
N_BLK = 16
N_GRP = 16


def plant(entries, rng, low, largest):
    index_at = [jax.random.randint(jax.random.fold_in(rng, axis), (), 0, length) for axis, length in enumerate(entries.shape)]
    longest = entries.shape.index(max(entries.shape))
    neighbour = index_at[:longest] + [(index_at[longest] + 1) % entries.shape[longest]] + index_at[longest + 1:]
    return entries.at[tuple(index_at)].set(low).at[tuple(neighbour)].set(largest)


def shard_levels(stream_key, shape, shards, smallest, top_value):
    def one(axis_at, shards_of):
        steps = jax.random.uniform(jax.random.fold_in(jax.random.fold_in(stream_key, 6), axis_at), (shards_of,), jnp.float32, smallest / len(shards), top_value / len(shards))
        return jnp.repeat(jnp.exp(steps), shape[axis_at] // shards_of).reshape((-1,) + (1,) * (len(shape) - axis_at - 1))

    loudness = one(*shards[0])
    for cut in shards[1:]:
        loudness = loudness * one(*cut)
    return loudness


def bell_draw(own_key, shape, scale, limit, shards=(), kind=jnp.bfloat16):
    drawn = scale * jax.random.normal(own_key, shape, jnp.float32)
    if shards:
        drawn = drawn * shard_levels(own_key, shape, shards, -0.22, 0.18)
    return jnp.clip(drawn, -limit, limit).astype(kind)


def setup_inputs(seed: int = 0) -> dict:
    key_of = jax.random.split(jax.random.key(seed), 8)
    img_feat = bell_draw(key_of[0], (NIMG, E), 1.0, 6.0, ((0, 256),))
    txt_feat = bell_draw(key_of[1], (NIMG, E), 1.0, 6.0, ((0, 256),))
    img_head = bell_draw(key_of[2], (E, D), E ** -0.5, 0.21875)
    txt_head = bell_draw(key_of[3], (E, D), E ** -0.5, 0.21875)
    logit_scale = jnp.clip(jnp.exp(jax.random.uniform(key_of[4], (1,), jnp.float32, math.log(5.0), math.log(15.0))), 5.0, 15.0)
    logit_bias = jnp.clip(jax.random.uniform(key_of[5], (1,), jnp.float32, -8.0, -4.0), -8.0, -4.0)
    pair_offset = plant(jax.random.randint(key_of[6], (NIMG,), 0, STEPS), jax.random.fold_in(key_of[6], 1), 0, STEPS - 1).astype(jnp.int32)
    return {"img_feat": img_feat, "txt_feat": txt_feat, "img_head": img_head, "txt_head": txt_head, "logit_scale": logit_scale, "logit_bias": logit_bias, "pair_offset": pair_offset}


def unit_rows(features, head):
    projected = jnp.dot(features, head, preferred_element_type=jnp.float32)
    length = jnp.sqrt(lax.optimization_barrier(jnp.sum(projected * projected, axis=-1, keepdims=True)) + 1e-06)
    return (projected / length, length)

def unit_grad(gradient, direction, length):
    inner = lax.optimization_barrier(jnp.sum(direction * gradient, axis=-1, keepdims=True))
    return ((gradient - direction * inner) / length).astype(jnp.bfloat16)

def reference(img_feat, txt_feat, img_head, txt_head, logit_scale, logit_bias, pair_offset):
    img_dir, img_len = unit_rows(img_feat, img_head)
    txt_dir, txt_len = unit_rows(txt_feat, txt_head)
    img_unit = img_dir.astype(jnp.bfloat16)
    txt_unit = txt_dir.astype(jnp.bfloat16)
    block_rows = ROWS * N_GRP
    blocks = N_BLK
    img_blocks = img_unit.reshape(blocks, block_rows, D)
    txt_blocks = txt_unit.reshape(blocks, block_rows, D)
    offset_blocks = pair_offset.reshape(blocks, block_rows)
    scored = jnp.concatenate([jnp.roll(txt_blocks, shift_by, axis=0) for shift_by in range(STEPS)], axis=1)
    temper = logit_scale[0]
    offset_bias = logit_bias[0]

    def block_terms(inputs):
        img_rows, texts, offsets = inputs
        logits = temper * jnp.dot(img_rows, texts.T, preferred_element_type=jnp.float32) + offset_bias
        columns = jnp.arange(STEPS * block_rows, dtype=jnp.int32)[None, :]
        target = offsets * block_rows + jnp.arange(block_rows, dtype=jnp.int32)
        labels = jnp.where(columns == target[:, None], 1.0, -1.0).astype(jnp.float32)
        row_loss = -lax.optimization_barrier(jnp.sum(jax.nn.log_sigmoid(labels * logits), axis=1))
        weight = (temper * -64.0 * labels * jax.nn.sigmoid(-labels * logits)).astype(jnp.bfloat16)
        img_part = jnp.dot(weight, texts, preferred_element_type=jnp.float32)
        txt_part = jnp.dot(weight.T, img_rows, preferred_element_type=jnp.float32)
        return (jnp.sum(row_loss), img_part, txt_part)
    losses, img_parts, txt_parts = lax.map(block_terms, (img_blocks, scored, offset_blocks))
    txt_parts = txt_parts.reshape(blocks, STEPS, block_rows, D)
    txt_total = jnp.zeros((blocks, block_rows, D), jnp.float32)
    for shift_by in range(STEPS):
        txt_total = txt_total + jnp.roll(txt_parts[:, shift_by], -shift_by, axis=0)
    img_grad = img_parts.reshape(NIMG, D)
    txt_grad = txt_total.reshape(NIMG, D)
    img_dgrad = unit_grad(img_grad, img_dir, img_len)
    txt_dgrad = unit_grad(txt_grad, txt_dir, txt_len)
    img_feat_grad = jnp.dot(img_dgrad, img_head.T, preferred_element_type=jnp.float32)
    txt_feat_grad = jnp.dot(txt_dgrad, txt_head.T, preferred_element_type=jnp.float32)
    norm_root = math.sqrt(NIMG)
    img_head_grad = jnp.dot(img_feat.T, img_dgrad, preferred_element_type=jnp.float32) / norm_root
    txt_head_grad = jnp.dot(txt_feat.T, txt_dgrad, preferred_element_type=jnp.float32) / norm_root
    mean_loss = (jnp.sum(losses) / NIMG).reshape(1)
    return (img_feat_grad, txt_feat_grad, img_head_grad, txt_head_grad, mean_loss)
```

```python
import math

import jax
import jax.numpy as jnp
from jax import lax
from jax.experimental import pallas as pl
from jax.experimental.pallas import tpu as pltpu
from jax.sharding import PartitionSpec as P

F32 = jnp.float32
BF16 = jnp.bfloat16
NT = (((1,), (1,)), ((), ()))
TN = (((0,), (0,)), ((), ()))
NN = (((1,), (0,)), ((), ()))
AXES = ("blk", "grp")
SIZES = (4, 2, 2, 4, 4)
X, ZH, CORE, ZL, Y = range(5)


def mm(a, b, dims):
    return lax.dot_general(a, b, dims, preferred_element_type=F32)


def coords():
    out = []
    for n in range(256):
        c = []
        for s in reversed(SIZES):
            c.append(n % s)
            n //= s
        out.append(tuple(reversed(c)))
    return out


def index_of(c):
    n = 0
    for s, v in zip(SIZES, c):
        n = n * s + v
    return n


def route(move):
    return [(index_of(c), index_of(move(list(c)))) for c in coords()]


def along(axis, distance):
    def move(c):
        c[axis] = (c[axis] + distance) % SIZES[axis]
        return c

    return route(move)


def by_core(first, second, distance):
    def move(c):
        axis = first if c[CORE] == 0 else second
        c[axis] = (c[axis] + distance) % SIZES[axis]
        return c

    return route(move)


def along_z(distance):
    def move(c):
        z = (c[ZH] * 4 + c[ZL] + distance) % 8
        c[ZH], c[ZL] = z // 4, z % 4
        return c

    return route(move)


def along_blk(distance):
    return [(i, (i + 16 * distance) % 256) for i in range(256)]


def send(x, pairs):
    return lax.ppermute(x, AXES, pairs)


def after(first, *others):
    return lax.optimization_barrier((first,) + others)


VMEM = pl.BlockSpec(memory_space=pltpu.VMEM)
SMEM = pl.BlockSpec(memory_space=pltpu.SMEM)


def call(kernel, outs, n_smem, n_vmem, scratch=()):
    return pl.pallas_call(
        kernel,
        out_shape=[jax.ShapeDtypeStruct(s, t) for s, t in outs],
        in_specs=[SMEM] * n_smem + [VMEM] * n_vmem,
        out_specs=[VMEM] * len(outs),
        scratch_shapes=list(scratch),
        compiler_params=pltpu.CompilerParams(vmem_limit_bytes=56 * 1024 * 1024),
    )


def main_kernel(rows, dim, *refs):
    (idx, scal, x0, x1, x2, x3, o0, o1, o2, o3, p0, p1, p2, p3, wi, wt, off) = refs[:17]
    gi, go, gp = refs[17:21], refs[21:25], refs[25:29]
    keep, other = refs[29:31]
    xs, ts, pi, pt, ui, ut, li, lt, lg, wgt, dg, acc = refs[31:]
    m = 4 * rows
    for k, r in enumerate((x0, x1, x2, x3)):
        xs[k * rows:(k + 1) * rows] = r[...]
    for k, r in enumerate((o0, o1, o2, o3, p0, p1, p2, p3)):
        ts[k * rows:(k + 1) * rows] = r[...]

    def lanes(v):
        total = v[:, 0:128]
        for k in range(1, dim // 128):
            total = total + v[:, k * 128:(k + 1) * 128]
        return jnp.sum(total, axis=-1, keepdims=True)

    def normalise(proj, direction, unit, inv, at):
        s = lax.rsqrt(lanes(proj * proj) + 1e-06)
        d = proj * s
        direction[at] = d
        unit[at] = d.astype(BF16)
        inv[at] = jnp.broadcast_to(s, (m, 128))

    def project(g, direction, inv, at):
        d = direction[at]
        s = inv[at][:, :1]
        inner = lanes(d * g)
        dg[at] = (g * s - d * (inner * s)).astype(BF16)

    whole = slice(0, m)
    sets = (slice(0, m), slice(m, 2 * m))
    normalise(mm(xs[...], wi[...], NN), pi, ui, li, whole)
    temper = scal[0]
    bias = scal[1]
    acc[...] = jnp.zeros_like(acc)
    for j, at in enumerate(sets):
        normalise(mm(ts[at], wt[...], NN), pt, ut, lt, at)
        lg[...] = mm(ui[...], ut[at], NT)

        def score(i, masked):
            here = pl.ds(pl.multiple_of(i * 64, 64), 64)
            l = temper * lg[here] + bias
            t = 64.0 * temper
            if masked:
                row = lax.broadcasted_iota(jnp.int32, (64, m), 0) + i * 64
                col = lax.broadcasted_iota(jnp.int32, (64, m), 1)
                pos = (row == col) & (off[here] == j)
                l = jnp.where(pos, -l, l)
                t = jnp.where(pos, -t, t)
            e = jnp.exp(l)
            u = 1.0 + e
            r = 1.0 / u
            terms = jnp.log(u) + (e - (u - 1.0)) * r
            total = terms[0:8]
            for k in range(1, 8):
                total = total + terms[k * 8:(k + 1) * 8]
            acc[...] += total
            wgt[here, at] = (t * (e * r)).astype(BF16)
            return 0

        lax.fori_loop(0, rows // 64, lambda i, _: score(i, True), 0)
        lax.fori_loop(rows // 64, m // 64, lambda i, _: score(i, False), 0)

    first = idx[0] == 0
    project(mm(wgt[...], ut[...], NN), pi, li, whole)
    for k, r in enumerate(gi):
        r[...] = dg[k * rows:(k + 1) * rows]
    himg = mm(xs[...], dg[whole], TN)
    loss = jnp.sum(acc[...])

    @pl.when(first)
    def _():
        keep[0:dim] = himg

    @pl.when(jnp.logical_not(first))
    def _():
        other[0:dim] = himg.astype(BF16)

    for at in sets:
        project(mm(wgt[:, at], ui[...], TN), pt, lt, at)
    for k, r in enumerate(tuple(go) + tuple(gp)):
        r[...] = dg[k * rows:(k + 1) * rows]
    htxt = mm(ts[...], dg[...], TN)

    @pl.when(first)
    def _():
        other[0:dim] = htxt.astype(BF16)

    @pl.when(jnp.logical_not(first))
    def _():
        keep[0:dim] = htxt

    mark = split_loss(jnp.full((8, dim), loss, F32), dim)
    keep[dim:dim + 16] = mark.astype(F32)
    other[dim:dim + 16] = mark


def split_loss(total, dim):
    hi = total.astype(BF16)
    lo = (total - hi.astype(F32)).astype(BF16)
    row = lax.broadcasted_iota(jnp.int32, (16, dim), 0)
    return jnp.where(row < 8, jnp.broadcast_to(hi[:1], (16, dim)).astype(F32), jnp.broadcast_to(lo[:1], (16, dim)).astype(F32)).astype(BF16)


def joined_loss(block, start):
    v = block[start:start + 16].astype(F32)
    return v[0:8] + v[8:16]


def core_sum_kernel(part, dim, idx, keep, recv, own, c1, c2, c3, mark):
    me = idx[1]
    at = pl.ds(pl.multiple_of(me * part, part), part)
    own[...] = keep[at] + recv[at].astype(F32)
    total = joined_loss(keep, 4 * part) + joined_loss(recv, 4 * part)
    loss = split_loss(total[:, 0:128], 128)
    mark[...] = loss
    for d, c in enumerate((c1, c2, c3), 1):
        at = pl.ds(pl.multiple_of(lax.rem(me + d, 4) * part, part), part)
        fold(c, (keep[at] + recv[at].astype(F32)).astype(BF16), loss)


def fold(out, block, loss):
    rows, dim = block.shape
    for k in range(dim // 128):
        out[k * rows:(k + 1) * rows] = block[:, k * 128:(k + 1) * 128]
    n = rows * (dim // 128)
    out[n:n + 16] = loss


def unfold(ref, rows, dim):
    n = dim // 128
    return jnp.concatenate([ref[k * rows:(k + 1) * rows].astype(F32) for k in range(n)], axis=1)


def ordered_loss(me, n, slots, mine, others, start):
    slots[me] = mine
    for d, r in others:
        slots[lax.rem(me + n - d, n)] = joined_loss(r, start)
    total = slots[0]
    for k in range(1, n):
        total = total + slots[k]
    return total


def stage_sum_kernel(part, small, dim, idx, own, mark, r1, r2, r3, own2, c1, c2, c3, mark2, full, slots):
    wide = dim // 128
    full[...] = own[...] + (unfold(r1, part, dim) + (unfold(r2, part, dim) + unfold(r3, part, dim)))
    total = ordered_loss(idx[1], 4, slots, joined_loss(mark, 0), ((1, r1), (2, r2), (3, r3)), part * wide)
    loss = split_loss(total, 128)
    mark2[...] = loss
    me = idx[2]
    own2[...] = full[pl.ds(pl.multiple_of(me * small, small), small)]
    for d, c in enumerate((c1, c2, c3), 1):
        at = pl.ds(pl.multiple_of(lax.rem(me + d, 4) * small, small), small)
        fold(c, full[at].astype(BF16), loss)


def second_sum_kernel(small, dim, idx, own, mark, r1, r2, r3, out, slots):
    total = own[...] + (unfold(r1, small, dim) + (unfold(r2, small, dim) + unfold(r3, small, dim)))
    loss = ordered_loss(idx[2], 4, slots, joined_loss(mark, 0), ((1, r1), (2, r2), (3, r3)), small * (dim // 128))
    fold(out, total.astype(BF16), split_loss(loss, 128))


def z_sum_kernel(small, dim, idx, mine, *refs):
    others, (out, mark, parts, slots) = refs[:7], refs[7:]
    me = idx[3]
    parts[me] = unfold(mine, small, dim)
    for d, r in enumerate(others, 1):
        parts[lax.rem(me + 8 - d, 8)] = unfold(r, small, dim)
    total = parts[0]
    for k in range(1, 8):
        total = total + parts[k]
    out[...] = total.astype(BF16)
    n = small * (dim // 128)
    loss = ordered_loss(me, 8, slots, joined_loss(mine, n), tuple(enumerate(others, 1)), n)
    mark[...] = split_loss(jnp.concatenate([loss] * (dim // 128), axis=1), dim)


def place_kernel(slot, part, extra, idx, *refs):
    pieces, out = refs[:4], refs[-1]
    me = idx[slot]
    for d, r in enumerate(pieces):
        out[pl.ds(pl.multiple_of(lax.rem(me + 4 - d, 4) * part, part), part)] = r[...]
    if extra:
        out[4 * part:4 * part + 16] = refs[4][...]


def finish_kernel(dim, norm_root, total_rows, idx, mine, theirs, img, txt, loss):
    first = idx[0] == 0
    scale = F32(1.0 / norm_root)

    @pl.when(first)
    def _():
        img[...] = mine[0:dim].astype(F32) * scale
        txt[...] = theirs[0:dim].astype(F32) * scale

    @pl.when(jnp.logical_not(first))
    def _():
        txt[...] = mine[0:dim].astype(F32) * scale
        img[...] = theirs[0:dim].astype(F32) * scale

    both = joined_loss(mine, dim) + joined_loss(theirs, dim)
    loss[...] = both[:, 0:128] * F32(0.5 / total_rows)


def feat_kernel(n, *refs):
    parts, head, out = refs[:n], refs[n], refs[n + 1]
    total = parts[0][...].astype(F32)
    for r in parts[1:]:
        total = total + r[...].astype(F32)
    out[...] = mm(total.astype(BF16), head[...], NT)


def sum_kernel(*refs):
    total = refs[0][...].astype(F32)
    for r in refs[1:-1]:
        total = total + r[...].astype(F32)
    refs[-1][...] = total.astype(BF16)


def body(img_feat, txt_feat, img_head, txt_head, logit_scale, logit_bias, pair_offset):
    rows, width = img_feat.shape
    dim = img_head.shape[1]
    blk, grp = lax.axis_index("blk"), lax.axis_index("grp")
    core, x, zh = blk % 2, blk // 4, (blk // 2) % 2
    zl, y = grp // 4, grp % 4
    idx = jnp.stack([core, jnp.where(core == 0, x, y), jnp.where(core == 0, y, x), zh * 4 + zl]).astype(jnp.int32)
    scal = jnp.concatenate([logit_scale, logit_bias])
    m = 4 * rows

    prev = send(txt_feat, along_blk(1))
    owns = [txt_feat] + [send(txt_feat, along(Y, -d)) for d in (1, 2, 3)]
    late, prev = after(img_feat, prev)
    imgs = [img_feat] + [send(late if d == 2 else img_feat, along(ZL, -d)) for d in (1, 2, 3)]
    prevs = [prev] + [send(prev, along(Y, -d)) for d in (1, 2, 3)]

    piece = ((rows, dim), BF16)
    outs = call(
        lambda *r: main_kernel(rows, dim, *r),
        [piece] * 12 + [((dim + 16, dim), F32), ((dim + 16, dim), BF16)],
        2,
        15,
        [
            pltpu.VMEM((m, width), BF16),
            pltpu.VMEM((2 * m, width), BF16),
            pltpu.VMEM((m, dim), F32),
            pltpu.VMEM((2 * m, dim), F32),
            pltpu.VMEM((m, dim), BF16),
            pltpu.VMEM((2 * m, dim), BF16),
            pltpu.VMEM((m, 128), F32),
            pltpu.VMEM((2 * m, 128), F32),
            pltpu.VMEM((m, m), F32),
            pltpu.VMEM((m, 2 * m), BF16),
            pltpu.VMEM((2 * m, dim), BF16),
            pltpu.VMEM((8, m), F32),
        ],
    )(idx, scal, *imgs, *owns, *prevs, img_head, txt_head, pair_offset.reshape(rows, 1))
    gi, go, gp, keep, other = outs[0:4], outs[4:8], outs[8:12], outs[12], outs[13]

    ri = [gi[0]] + [send(gi[d], along(ZL, d)) for d in (1, 2, 3)]
    recv = send(other, along(CORE, 1))
    part, small, wide = dim // 4, dim // 16, dim // 128
    loss_block = ((16, 128), BF16)
    slots = pltpu.VMEM((4, 8, 128), F32)
    own1, a1, a2, a3, mark1 = call(
        lambda *r: core_sum_kernel(part, dim, *r),
        [((part, dim), F32)] + [((part * wide + 16, 128), BF16)] * 3 + [loss_block],
        1,
        2,
    )(idx, keep, recv)
    got = [send(a, by_core(X, Y, d)) for d, a in ((1, a1), (2, a2), (3, a3))]
    *gq, got0, got1, got2 = after(*gp, *go, *got)
    gp, go, got = gq[0:4], gq[4:8], [got0, got1, got2]
    own2, b1, b2, b3, mark2 = call(
        lambda *r: stage_sum_kernel(part, small, dim, *r),
        [((small, dim), F32)] + [((small * wide + 16, 128), BF16)] * 3 + [loss_block],
        1,
        5,
        [pltpu.VMEM((part, dim), F32), slots],
    )(idx, own1, mark1, *got)
    rp = [gp[0]] + [send(gp[d], along(Y, d)) for d in (1, 2, 3)]
    got = [send(b, by_core(Y, X, d)) for d, b in ((1, b1), (2, b2), (3, b3))]
    (zpart,) = call(
        lambda *r: second_sum_kernel(small, dim, *r), [((small * wide + 16, 128), BF16)], 1, 5, [slots]
    )(idx, own2, mark2, *got)
    ro = [go[0]] + [send(go[d], along(Y, d)) for d in (1, 2, 3)]
    zpart, *ri = after(zpart, *ri)
    got = [send(zpart, along_z(d)) for d in range(1, 8)]
    (img_feat_grad,) = call(lambda *r: feat_kernel(4, *r), [((rows, width), F32)], 0, 5)(*ri, img_head)
    (back,) = call(sum_kernel, [((rows, dim), BF16)], 0, 4)(*rp)
    done, mark3 = call(
        lambda *r: z_sum_kernel(small, dim, *r),
        [((small, dim), BF16), ((16, dim), BF16)],
        1,
        8,
        [pltpu.VMEM((8, small, dim), F32), pltpu.VMEM((8, 8, 128), F32)],
    )(idx, zpart, *got)
    done, img_feat_grad, back = after(done, img_feat_grad, back)
    back = send(back, along_blk(-1))
    got = [done] + [send(done, by_core(Y, X, d)) for d in (1, 2, 3)]
    (quarter,) = call(lambda *r: place_kernel(2, small, False, *r), [((part, dim), BF16)], 1, 4)(idx, *got)
    quarter, *ro = after(quarter, *ro)
    got = [quarter] + [send(quarter, by_core(X, Y, d)) for d in (1, 2, 3)]
    (whole,) = call(lambda *r: place_kernel(1, part, True, *r), [((dim + 16, dim), BF16)], 1, 5)(idx, *got, mark3)
    whole, back = after(whole, back)
    theirs = send(whole, along(CORE, 1))
    (txt_feat_grad,) = call(lambda *r: feat_kernel(5, *r), [((rows, width), F32)], 0, 6)(*ro, back, txt_head)
    total_rows = rows * 256
    img_head_grad, txt_head_grad, loss = call(
        lambda *r: finish_kernel(dim, math.sqrt(total_rows), total_rows, *r),
        [((dim, dim), F32)] * 2 + [((8, 128), F32)],
        1,
        2,
    )(idx, whole, theirs)

    return img_feat_grad, txt_feat_grad, img_head_grad, txt_head_grad, loss[0, 0:1]


def solution(mesh):
    rows = P(AXES, None)
    in_specs = (rows, rows, P(), P(), P(), P(), P(AXES))
    out_specs = (rows, rows, P(), P(), P())
    return jax.shard_map(body, mesh=mesh, in_specs=in_specs, out_specs=out_specs, check_vma=False)
```

```python
import math

import jax
import jax.numpy as jnp
from jax import lax
from jax.experimental import pallas as pl
from jax.experimental.pallas import tpu as pltpu
from jax.sharding import PartitionSpec as P

F32 = jnp.float32
BF16 = jnp.bfloat16
NT = (((1,), (1,)), ((), ()))
TN = (((0,), (0,)), ((), ()))
NN = (((1,), (0,)), ((), ()))
AXES = ("blk", "grp")
SIZES = (4, 2, 2, 4, 4)
X, ZH, CORE, ZL, Y = range(5)


def mm(a, b, dims):
    return lax.dot_general(a, b, dims, preferred_element_type=F32)


def coords():
    out = []
    for n in range(256):
        c = []
        for s in reversed(SIZES):
            c.append(n % s)
            n //= s
        out.append(tuple(reversed(c)))
    return out


def index_of(c):
    n = 0
    for s, v in zip(SIZES, c):
        n = n * s + v
    return n


def route(move):
    return [(index_of(c), index_of(move(list(c)))) for c in coords()]


def along(axis, distance):
    def move(c):
        c[axis] = (c[axis] + distance) % SIZES[axis]
        return c

    return route(move)


def by_core(first, second, distance):
    def move(c):
        axis = first if c[CORE] == 0 else second
        c[axis] = (c[axis] + distance) % SIZES[axis]
        return c

    return route(move)


def across_z(bit):
    def move(c):
        c[ZL] = c[ZL] ^ bit
        return c

    return route(move)


def along_blk(distance):
    return [(i, (i + 16 * distance) % 256) for i in range(256)]


def send(x, pairs):
    return lax.ppermute(x, AXES, pairs)


def after(first, *others):
    return lax.optimization_barrier((first,) + others)


VMEM = pl.BlockSpec(memory_space=pltpu.VMEM)
SMEM = pl.BlockSpec(memory_space=pltpu.SMEM)


def call(kernel, outs, n_smem, n_vmem, scratch=(), limit=16, placed=True):
    def here(shape, dtype):
        if placed and len(shape) > 1:
            return pltpu.VMEM(shape, dtype)
        return jax.ShapeDtypeStruct(shape, dtype)

    run = pl.pallas_call(
        kernel,
        out_shape=[here(s, t) for s, t in outs],
        in_specs=[SMEM] * n_smem + [VMEM] * n_vmem,
        out_specs=[SMEM if len(s) == 1 else VMEM for s, _ in outs],
        scratch_shapes=list(scratch),
        compiler_params=pltpu.CompilerParams(vmem_limit_bytes=limit * 1024 * 1024),
    )

    def launch(*args):
        held = [
            pltpu.with_memory_space_constraint(a[0], pltpu.HBM)
            if isinstance(a, list)
            else pltpu.with_memory_space_constraint(a, pltpu.VMEM)
            for a in args[n_smem:]
        ]
        return run(*args[:n_smem], *held)

    return launch


def lanes(v):
    total = v[:, 0:128]
    for k in range(1, v.shape[1] // 128):
        total = total + v[:, k * 128:(k + 1) * 128]
    return jnp.sum(total, axis=-1, keepdims=True)


def normalise(proj, direction, unit, inv, at):
    s = lax.rsqrt(lanes(proj * proj) + 1e-06)
    d = proj * s
    direction[...] = d
    unit[at] = d.astype(BF16)
    inv[...] = jnp.broadcast_to(s, inv.shape)


def project(g, direction, inv):
    d = direction[...]
    s = inv[...][:, :1]
    inner = lanes(d * g)
    return (g * s - d * (inner * s)).astype(BF16)


def score(lg, wgt, acc, scal, down, right, marked=0, which=None):
    n, columns = lg.shape
    temper, bias = scal[0][0], scal[1][0]
    if marked:
        off, here_set = which
        wanted = jnp.concatenate([off[...], jnp.full((1, columns - marked), -1, jnp.int32)], axis=1) == here_set

    def step(i, masked):
        here = pl.ds(pl.multiple_of(i * 64, 64), 64)
        l = temper * lg[here] + bias
        t = 64.0 * temper
        if masked:
            row = lax.broadcasted_iota(jnp.int32, (64, columns), 0) + i * 64
            col = lax.broadcasted_iota(jnp.int32, (64, columns), 1)
            pos = (col == row) & wanted
            l = jnp.where(pos, -l, l)
            t = jnp.where(pos, -t, t)
        e = jnp.exp(l)
        u = 1.0 + e
        r = 1.0 / u
        terms = jnp.log(u) + (e - (u - 1.0)) * r
        total = terms[0:8]
        for k in range(1, 8):
            total = total + terms[k * 8:(k + 1) * 8]
        acc[:, 0:columns] += total
        there = pl.ds(pl.multiple_of(down + i * 64, 64), 64)
        wgt[there, right:right + columns] = (t * (e * r)).astype(BF16)
        return 0

    if marked:
        lax.fori_loop(0, marked // 64, lambda i, _: step(i, True), 0)
    lax.fori_loop(marked // 64, n // 64, lambda i, _: step(i, False), 0)


def first_kernel(rows, temper, bias, x0, x1, x2, x3, t0, t1, wi, wt, off, xs, ts, pi, ui, li, pt, ut, lt, wgt, acc, lg):
    for k, r in enumerate((x0, x1, x2, x3)):
        xs[k * rows:(k + 1) * rows] = r[...]
    for k, r in enumerate((t0, t1)):
        ts[k * rows:(k + 1) * rows] = r[...]
    normalise(mm(ts[...], wt[...], NN), pt, ut, lt, slice(None))
    normalise(mm(xs[...], wi[...], NN), pi, ui, li, slice(None))
    lg[...] = mm(ui[...], ut[...], NT)
    acc[...] = jnp.zeros_like(acc)
    score(lg, wgt, acc, (temper, bias), 0, 0, rows, (off, 0))


def main_kernel(rows, dim, *refs):
    idx, scal, (xs0, ts0, pi0, ui0, li0, pt0, ut0, lt0, wgt0, acc0) = refs[0], refs[1:3], refs[3:13]
    images, texts, (wi, wt, off) = refs[13:17], refs[17:19], refs[19:22]
    g0, g1, g3, g2a, g2b, gt_own, gt_out, keep, other = refs[22:31]
    xs, ts, pi1, pt1, ui, ut, li1, lt1, lg, lh, wgt, dg, acc = refs[31:]
    m, h = 4 * rows, 2 * rows
    top, low = slice(0, m), slice(m, 2 * m)
    front, rear = slice(0, h), slice(h, m)
    xs[top] = xs0[...]
    ui[top] = ui0[...]
    ts[front] = ts0[...]
    ut[front] = ut0[...]
    wgt[top, 0:h] = wgt0[...]
    acc[:, 0:h] = acc0[...]
    acc[:, h:m] = jnp.zeros_like(acc0)
    for k, r in enumerate(images):
        xs[m + k * rows:m + (k + 1) * rows] = r[...]
    for k, r in enumerate(texts):
        ts[h + k * rows:h + (k + 1) * rows] = r[...]

    normalise(mm(ts[rear], wt[...], NN), pt1, ut, lt1, rear)
    lh[...] = mm(ui[top], ut[rear], NT)
    score(lh, wgt, acc, scal, 0, h, rows, (off, 1))
    normalise(mm(xs[low], wi[...], NN), pi1, ui, li1, low)
    lg[...] = mm(ui[low], ut[...], NT)
    score(lg, wgt, acc, scal, m, 0)
    loss = jnp.sum(acc[...])

    first = idx[0] == 0
    grad = mm(wgt[...], ui[...], TN)
    dg[front] = project(grad[front], pt0, lt0)
    dg[rear] = project(grad[rear], pt1, lt1)
    for out, which in ((gt_own, 0), (gt_out, 1)):
        out[0:rows] = dg[which * rows:(which + 1) * rows]
        out[rows:2 * rows] = dg[(which + 2) * rows:(which + 3) * rows]
    htxt = mm(ts[...], dg[top], TN)

    @pl.when(first)
    def _():
        other[0:dim] = htxt.astype(BF16)

    @pl.when(jnp.logical_not(first))
    def _():
        keep[0:dim] = htxt

    dg[top] = project(mm(wgt[top], ut[...], NN), pi0, li0)
    dg[low] = project(mm(wgt[low], ut[...], NN), pi1, li1)
    for k, r in ((0, g0), (1, g1), (3, g3)):
        r[0:rows] = dg[k * rows:(k + 1) * rows]
        r[rows:2 * rows] = dg[(k + 4) * rows:(k + 5) * rows]
    g2a[...] = dg[2 * rows:3 * rows]
    g2b[...] = dg[6 * rows:7 * rows]
    himg = mm(xs[...], dg[...], TN)

    @pl.when(first)
    def _():
        keep[0:dim] = himg

    @pl.when(jnp.logical_not(first))
    def _():
        other[0:dim] = himg.astype(BF16)

    mark = split_loss(jnp.full((8, dim), loss, F32), dim)
    keep[dim:dim + 16] = mark.astype(F32)
    other[dim:dim + 16] = mark


def split_loss(total, dim):
    hi = total.astype(BF16)
    lo = (total - hi.astype(F32)).astype(BF16)
    row = lax.broadcasted_iota(jnp.int32, (16, dim), 0)
    return jnp.where(row < 8, jnp.broadcast_to(hi[:1], (16, dim)).astype(F32), jnp.broadcast_to(lo[:1], (16, dim)).astype(F32)).astype(BF16)


def joined_loss(block, start):
    v = block[start:start + 16].astype(F32)
    return v[0:8] + v[8:16]


def core_sum_kernel(part, dim, idx, keep, recv, own, c1, c2, c3, mark):
    me = idx[1]
    at = pl.ds(pl.multiple_of(me * part, part), part)
    own[...] = keep[at] + recv[at].astype(F32)
    total = joined_loss(keep, 4 * part) + joined_loss(recv, 4 * part)
    loss = split_loss(total[:, 0:128], 128)
    mark[...] = loss
    for d, c in enumerate((c1, c2, c3), 1):
        at = pl.ds(pl.multiple_of(lax.rem(me + d, 4) * part, part), part)
        fold(c, (keep[at] + recv[at].astype(F32)).astype(BF16), loss)


def fold(out, block, loss):
    rows, dim = block.shape
    for k in range(dim // 128):
        out[k * rows:(k + 1) * rows] = block[:, k * 128:(k + 1) * 128]
    n = rows * (dim // 128)
    out[n:n + 16] = loss


def unfold(ref, rows, dim):
    n = dim // 128
    return jnp.concatenate([ref[k * rows:(k + 1) * rows].astype(F32) for k in range(n)], axis=1)


def ordered_loss(me, n, slots, mine, others, start):
    slots[me] = mine
    for d, r in others:
        slots[lax.rem(me + n - d, n)] = joined_loss(r, start)
    total = slots[0]
    for k in range(1, n):
        total = total + slots[k]
    return total


def stage_sum_kernel(part, small, dim, idx, own, mark, r1, r2, r3, own2, c1, c2, c3, mark2, full, slots):
    wide = dim // 128
    full[...] = own[...] + (unfold(r1, part, dim) + (unfold(r2, part, dim) + unfold(r3, part, dim)))
    total = ordered_loss(idx[1], 4, slots, joined_loss(mark, 0), ((1, r1), (2, r2), (3, r3)), part * wide)
    loss = split_loss(total, 128)
    mark2[...] = loss
    me = idx[2]
    own2[...] = full[pl.ds(pl.multiple_of(me * small, small), small)]
    for d, c in enumerate((c1, c2, c3), 1):
        at = pl.ds(pl.multiple_of(lax.rem(me + d, 4) * small, small), small)
        fold(c, full[at].astype(BF16), loss)


def second_sum_kernel(small, dim, idx, own, mark, r1, r2, r3, out, slots):
    total = own[...] + (unfold(r1, small, dim) + (unfold(r2, small, dim) + unfold(r3, small, dim)))
    loss = ordered_loss(idx[2], 4, slots, joined_loss(mark, 0), ((1, r1), (2, r2), (3, r3)), small * (dim // 128))
    fold(out, total.astype(BF16), split_loss(loss, 128))


def line_sum_kernel(small, dim, idx, mine, r1, r2, r3, out, parts, slots):
    me = idx[3]
    others = ((1, r1), (2, r2), (3, r3))
    parts[me] = unfold(mine, small, dim)
    for d, r in others:
        parts[lax.rem(me + 4 - d, 4)] = unfold(r, small, dim)
    total = (parts[0] + parts[1]) + (parts[2] + parts[3])
    n = small * (dim // 128)
    loss = ordered_loss(me, 4, slots, joined_loss(mine, n), others, n)
    fold(out, total.astype(BF16), split_loss(loss, 128))


def pair_sum_kernel(small, dim, mine, recv, out, mark):
    out[...] = (unfold(mine, small, dim) + unfold(recv, small, dim)).astype(BF16)
    n = small * (dim // 128)
    loss = joined_loss(mine, n) + joined_loss(recv, n)
    mark[...] = split_loss(jnp.concatenate([loss] * (dim // 128), axis=1), dim)


def quarter_kernel(small, idx, *refs):
    pieces, out = refs[:4], refs[4]
    for d, r in enumerate(pieces):
        out[pl.ds(pl.multiple_of(lax.rem(idx[2] + 4 - d, 4) * small, small), small)] = r[...]


def whole_kernel(part, idx, *refs):
    pieces, mark, out = refs[:4], refs[4], refs[5]
    for d, r in enumerate(pieces):
        out[pl.ds(pl.multiple_of(lax.rem(idx[1] + 4 - d, 4) * part, part), part)] = r[...]
    out[4 * part:4 * part + 16] = mark[...]


def finish_kernel(dim, norm_root, total_rows, idx, mine, theirs, img, txt, loss):
    first = idx[0] == 0
    scale = F32(1.0 / norm_root)

    @pl.when(first)
    def _():
        img[...] = mine[0:dim].astype(F32) * scale
        txt[...] = theirs[0:dim].astype(F32) * scale

    @pl.when(jnp.logical_not(first))
    def _():
        txt[...] = mine[0:dim].astype(F32) * scale
        img[...] = theirs[0:dim].astype(F32) * scale

    both = joined_loss(mine, dim) + joined_loss(theirs, dim)
    loss[0] = jnp.max(both[:, 0:128]) * F32(0.5 / total_rows)


def relay_kernel(rows, g1, g3, from_left, from_right, to_right, to_left):
    to_right[0:rows] = (g1[0:rows].astype(F32) + from_left[...].astype(F32)).astype(BF16)
    to_right[rows:2 * rows] = g1[rows:2 * rows]
    to_left[0:rows] = g3[0:rows]
    to_left[rows:2 * rows] = (g3[rows:2 * rows].astype(F32) + from_right[...].astype(F32)).astype(BF16)


def image_sum_kernel(rows, g0, left, right, own, out):
    total = g0[...].astype(F32) + (left[...].astype(F32) + right[...].astype(F32))
    own[...] = total[0:rows]
    out[...] = total[rows:2 * rows].astype(BF16)


def text_sum_kernel(rows, mine, recv, own, out):
    total = mine[...].astype(F32) + recv[...].astype(F32)
    own[...] = total[0:rows]
    out[...] = total[rows:2 * rows].astype(BF16)


def feat_kernel(own, recv, head, out):
    out[...] = mm((own[...] + recv[...].astype(F32)).astype(BF16), head[...], NT)


def body(img_feat, txt_feat, img_head, txt_head, logit_scale, logit_bias, pair_offset):
    rows, width = img_feat.shape
    dim = img_head.shape[1]
    blk, grp = lax.axis_index("blk"), lax.axis_index("grp")
    core, x, zh = blk % 2, blk // 4, (blk // 2) % 2
    zl, y = grp // 4, grp % 4
    idx = jnp.stack([core, jnp.where(core == 0, x, y), jnp.where(core == 0, y, x), zl]).astype(jnp.int32)
    m = 4 * rows

    h = 2 * rows
    off = pair_offset.reshape(1, rows)
    idx, off, img_feat, txt_feat = after(idx, off, img_feat, txt_feat)
    far = send(img_feat, across_z(2))
    near = [img_feat] + [send(img_feat, along(Y, -d)) for d in (1, 2, 3)]
    later, near[1] = after(txt_feat, near[1])
    prev = send(later, along_blk(1))
    own_pair = [txt_feat, send(txt_feat, across_z(1))]
    far, *near = after(far, *near)
    distant = [far] + [send(far, along(Y, -d)) for d in (1, 2, 3)]
    begun = call(
        lambda *r: first_kernel(rows, *r),
        [
            ((m, width), BF16),
            ((h, width), BF16),
            ((m, dim), F32),
            ((m, dim), BF16),
            ((m, 128), F32),
            ((h, dim), F32),
            ((h, dim), BF16),
            ((h, 128), F32),
            ((m, h), BF16),
            ((8, h), F32),
        ],
        2,
        9,
        [pltpu.VMEM((m, h), F32)],
        24,
    )(logit_scale, logit_bias, [near[0]], *near[1:], [own_pair[0]], own_pair[1], [img_head], [txt_head], [off])
    begun = list(begun)
    prev, begun[9] = after(prev, begun[9])
    prev_pair = [prev, send(prev, across_z(1))]

    pair = ((2 * rows, dim), BF16)
    outs = call(
        lambda *r: main_kernel(rows, dim, *r),
        [pair] * 3 + [((rows, dim), BF16)] * 2 + [pair] * 2 + [((dim + 16, dim), F32), ((dim + 16, dim), BF16)],
        3,
        19,
        [
            pltpu.VMEM((2 * m, width), BF16),
            pltpu.VMEM((m, width), BF16),
            pltpu.VMEM((m, dim), F32),
            pltpu.VMEM((h, dim), F32),
            pltpu.VMEM((2 * m, dim), BF16),
            pltpu.VMEM((m, dim), BF16),
            pltpu.VMEM((m, 128), F32),
            pltpu.VMEM((h, 128), F32),
            pltpu.VMEM((m, m), F32),
            pltpu.VMEM((m, h), F32),
            pltpu.VMEM((2 * m, m), BF16),
            pltpu.VMEM((2 * m, dim), BF16),
            pltpu.VMEM((8, m), F32),
        ],
        36,
    )(idx, logit_scale, logit_bias, *begun, *distant, *prev_pair, [img_head], [txt_head], [off])
    g0, g1, g3, g2a, g2b, gt_own, gt_out, keep, other = outs

    recv = send(other, along(CORE, 1))
    gt_in = send(gt_out, across_z(1))
    part, small, wide = dim // 4, dim // 16, dim // 128
    loss_block = ((16, 128), BF16)
    slots = pltpu.VMEM((4, 8, 128), F32)
    folded = ((small * wide + 16, 128), BF16)
    half = [((rows, dim), F32), ((rows, dim), BF16)]
    own1, a1, a2, a3, mark1 = call(
        lambda *r: core_sum_kernel(part, dim, *r),
        [((part, dim), F32)] + [((part * wide + 16, 128), BF16)] * 3 + [loss_block],
        1,
        2,
    )(idx, keep, recv)
    got = [send(a, by_core(X, Y, d)) for d, a in ((1, a1), (2, a2), (3, a3))]
    *got, gt_in = after(*got, gt_in)
    own2, b1, b2, b3, mark2 = call(
        lambda *r: stage_sum_kernel(part, small, dim, *r),
        [((small, dim), F32)] + [folded] * 3 + [loss_block],
        1,
        5,
        [pltpu.VMEM((part, dim), F32), slots],
    )(idx, own1, mark1, *got)
    txt_own, txt_out = call(lambda *r: text_sum_kernel(rows, *r), half, 0, 2)(gt_own, gt_in)
    back = send(txt_out, along_blk(-1))
    got = [send(b, by_core(Y, X, d)) for d, b in ((1, b1), (2, b2), (3, b3))]
    (zpart,) = call(lambda *r: second_sum_kernel(small, dim, *r), [folded], 1, 5, [slots])(idx, own2, mark2, *got)
    zpart, back, g2a, g2b = after(zpart, back, g2a, g2b)
    got = [send(zpart, along(ZL, d)) for d in (1, 2, 3)]
    from_left, from_right = send(g2a, along(Y, 1)), send(g2b, along(Y, -1))
    (zline,) = call(
        lambda *r: line_sum_kernel(small, dim, *r), [folded], 1, 4, [pltpu.VMEM((4, small, dim), F32), slots]
    )(idx, zpart, *got)
    zline, from_left, from_right = after(zline, from_left, from_right)
    zrecv = send(zline, along(ZH, 1))
    to_right, to_left = call(lambda *r: relay_kernel(rows, *r), [pair] * 2, 0, 4)(g1, g3, from_left, from_right)
    left, right = send(to_right, along(Y, 1)), send(to_left, along(Y, -1))
    done, mark3 = call(
        lambda *r: pair_sum_kernel(small, dim, *r), [((small, dim), BF16), ((16, dim), BF16)], 0, 2
    )(zline, zrecv)
    got = [done] + [send(done, by_core(Y, X, d)) for d in (1, 2, 3)]
    (quarter,) = call(lambda *r: quarter_kernel(small, *r), [((part, dim), BF16)], 1, 4)(idx, *got)
    quarter, left, right = after(quarter, left, right)
    img_own, img_out = call(lambda *r: image_sum_kernel(rows, *r), half, 0, 3)(g0, left, right)
    img_in = send(img_out, across_z(2))
    got = [quarter] + [send(quarter, by_core(X, Y, d)) for d in (1, 2, 3)]
    (txt_feat_grad,) = call(feat_kernel, [((rows, width), F32)], 0, 3, placed=False)(txt_own, back, [txt_head])
    (whole,) = call(lambda *r: whole_kernel(part, *r), [((dim + 16, dim), BF16)], 1, 5)(idx, *got, mark3)
    whole, txt_feat_grad, img_in = after(whole, txt_feat_grad, img_in)
    theirs = send(whole, along(CORE, 1))
    (img_feat_grad,) = call(feat_kernel, [((rows, width), F32)], 0, 3, placed=False)(img_own, img_in, [img_head])
    total_rows = rows * 256
    img_head_grad, txt_head_grad, loss = call(
        lambda *r: finish_kernel(dim, math.sqrt(total_rows), total_rows, *r),
        [((dim, dim), F32)] * 2 + [((1,), F32)],
        1,
        2,
        placed=False,
    )(idx, whole, theirs)

    return img_feat_grad, txt_feat_grad, img_head_grad, txt_head_grad, loss


def solution(mesh):
    rows = P(AXES, None)
    in_specs = (rows, rows, P(), P(), P(), P(), P(AXES))
    out_specs = (rows, rows, P(), P(), P())
    return jax.shard_map(body, mesh=mesh, in_specs=in_specs, out_specs=out_specs, check_vma=False)
```

```python
import math

import jax
import jax.numpy as jnp
from jax import lax
from jax.experimental import pallas as pl
from jax.experimental.pallas import tpu as pltpu
from jax.sharding import PartitionSpec as P

F32 = jnp.float32
BF16 = jnp.bfloat16
NT = (((1,), (1,)), ((), ()))
TN = (((0,), (0,)), ((), ()))
NN = (((1,), (0,)), ((), ()))
AXES = ("blk", "grp")
SIZES = (4, 2, 2, 4, 4)
X, ZH, CORE, ZL, Y = range(5)


def mm(a, b, dims):
    return lax.dot_general(a, b, dims, preferred_element_type=F32)


def coords():
    out = []
    for n in range(256):
        c = []
        for s in reversed(SIZES):
            c.append(n % s)
            n //= s
        out.append(tuple(reversed(c)))
    return out


def index_of(c):
    n = 0
    for s, v in zip(SIZES, c):
        n = n * s + v
    return n


def route(move):
    return [(index_of(c), index_of(move(list(c)))) for c in coords()]


def along(axis, distance):
    def move(c):
        c[axis] = (c[axis] + distance) % SIZES[axis]
        return c

    return route(move)


def by_core(first, second, distance):
    def move(c):
        axis = first if c[CORE] == 0 else second
        c[axis] = (c[axis] + distance) % SIZES[axis]
        return c

    return route(move)


def along_blk(distance):
    return [(i, (i + 16 * distance) % 256) for i in range(256)]


def across_z(bit, pairs=None):
    def move(c):
        c[ZL] = c[ZL] ^ bit
        return c

    turn = dict(route(move))
    return [(i, turn[j]) for i, j in (pairs or [(n, n) for n in range(256)])]


def send(x, pairs):
    return lax.ppermute(x, AXES, pairs)


def after(first, *others):
    return lax.optimization_barrier((first,) + others)


VMEM = pl.BlockSpec(memory_space=pltpu.VMEM)
SMEM = pl.BlockSpec(memory_space=pltpu.SMEM)


def call(kernel, outs, n_smem, n_vmem, scratch=(), limit=16, placed=True):
    def here(shape, dtype):
        if placed and len(shape) > 1:
            return pltpu.VMEM(shape, dtype)
        return jax.ShapeDtypeStruct(shape, dtype)

    run = pl.pallas_call(
        kernel,
        out_shape=[here(s, t) for s, t in outs],
        in_specs=[SMEM] * n_smem + [VMEM] * n_vmem,
        out_specs=[SMEM if len(s) == 1 else VMEM for s, _ in outs],
        scratch_shapes=list(scratch),
        compiler_params=pltpu.CompilerParams(vmem_limit_bytes=limit * 1024 * 1024),
    )

    def launch(*args):
        held = [
            pltpu.with_memory_space_constraint(a[0], pltpu.HBM)
            if isinstance(a, list)
            else pltpu.with_memory_space_constraint(a, pltpu.VMEM)
            for a in args[n_smem:]
        ]
        return run(*args[:n_smem], *held)

    return launch


def lanes(v):
    total = v[:, 0:128]
    for k in range(1, v.shape[1] // 128):
        total = total + v[:, k * 128:(k + 1) * 128]
    return jnp.sum(total, axis=-1, keepdims=True)


def normalise(proj, direction, unit, inv, at):
    s = lax.rsqrt(lanes(proj * proj) + 1e-06)
    d = proj * s
    direction[...] = d
    unit[at] = d.astype(BF16)
    inv[...] = jnp.broadcast_to(s, inv.shape)


def project(g, direction, inv):
    d = direction[...]
    s = inv[...][:, :1]
    inner = lanes(d * g)
    return (g * s - d * (inner * s)).astype(BF16)


def score(lg, wgt, acc, scal, down, right, marked=0, which=None):
    n, columns = lg.shape
    temper, bias = scal[0][0], scal[1][0]
    if marked:
        off, here_set = which
        wanted = jnp.concatenate([off[...], jnp.full((1, columns - marked), -1, jnp.int32)], axis=1) == here_set

    def step(i, masked):
        here = pl.ds(pl.multiple_of(i * 64, 64), 64)
        l = temper * lg[here] + bias
        t = 64.0 * temper
        if masked:
            row = lax.broadcasted_iota(jnp.int32, (64, columns), 0) + i * 64
            col = lax.broadcasted_iota(jnp.int32, (64, columns), 1)
            pos = (col == row) & wanted
            l = jnp.where(pos, -l, l)
            t = jnp.where(pos, -t, t)
        e = jnp.exp(l)
        u = 1.0 + e
        r = 1.0 / u
        terms = jnp.log(u) + (e - (u - 1.0)) * r
        total = terms[0:8]
        for k in range(1, 8):
            total = total + terms[k * 8:(k + 1) * 8]
        acc[:, 0:columns] += total
        there = pl.ds(pl.multiple_of(down + i * 64, 64), 64)
        wgt[there, right:right + columns] = (t * (e * r)).astype(BF16)
        return 0

    if marked:
        lax.fori_loop(0, marked // 64, lambda i, _: step(i, True), 0)
    lax.fori_loop(marked // 64, n // 64, lambda i, _: step(i, False), 0)


def first_kernel(rows, temper, bias, x0, x1, x2, x3, t0, t1, wi, wt, off, *refs):
    xs, ts, pi, ui, li, pt, ut, lt, wgt, acc, wi_out, wt_out, lg = refs
    for k, r in enumerate((x0, x1, x2, x3)):
        xs[k * rows:(k + 1) * rows] = r[...]
    for k, r in enumerate((t0, t1)):
        ts[k * rows:(k + 1) * rows] = r[...]
    wi_out[...] = wi[...]
    wt_out[...] = wt[...]
    normalise(mm(ts[...], wt[...], NN), pt, ut, lt, slice(None))
    normalise(mm(xs[...], wi[...], NN), pi, ui, li, slice(None))
    lg[...] = mm(ui[...], ut[...], NT)
    acc[...] = jnp.zeros_like(acc)
    score(lg, wgt, acc, (temper, bias), 0, 0, rows, (off, 0))


def second_kernel(rows, temper, bias, ui, t0, t1, wt, off, ts, pt, ut, lt, wgt, acc, lg):
    for k, r in enumerate((t0, t1)):
        ts[k * rows:(k + 1) * rows] = r[...]
    normalise(mm(ts[...], wt[...], NN), pt, ut, lt, slice(None))
    lg[...] = mm(ui[...], ut[...], NT)
    acc[...] = jnp.zeros_like(acc)
    score(lg, wgt, acc, (temper, bias), 0, 0, rows, (off, 1))


def main_kernel(rows, dim, *refs):
    idx, scal, (xs0, ts0, pi0, ui0, li0, pt0, ut0, lt0, wgt0, acc0, wi) = refs[0], refs[1:3], refs[3:14]
    (ts1, pt1, ut1, lt1, wgt1, acc1), images = refs[14:20], refs[20:24]
    g0, g1, g3, g2a, g2b, keep, other = refs[24:31]
    text_grads = refs[31:35]
    xs, ts, pi1, ui, ut, li1, lg, wgt, dg, acc = refs[35:]
    m, h = 4 * rows, 2 * rows
    top, low = slice(0, m), slice(m, 2 * m)
    front, rear = slice(0, h), slice(h, m)
    xs[top] = xs0[...]
    ui[top] = ui0[...]
    ts[front] = ts0[...]
    ts[rear] = ts1[...]
    ut[front] = ut0[...]
    ut[rear] = ut1[...]
    wgt[top, 0:h] = wgt0[...]
    wgt[top, h:m] = wgt1[...]
    acc[:, 0:h] = acc0[...]
    acc[:, h:m] = acc1[...]
    for k, r in enumerate(images):
        xs[m + k * rows:m + (k + 1) * rows] = r[...]

    normalise(mm(xs[low], wi[...], NN), pi1, ui, li1, low)
    lg[...] = mm(ui[low], ut[...], NT)
    score(lg, wgt, acc, scal, m, 0)
    loss = jnp.sum(acc[...])

    first = idx[0] == 0
    grad = mm(wgt[...], ui[...], TN)
    dg[front] = project(grad[front], pt0, lt0)
    dg[rear] = project(grad[rear], pt1, lt1)
    for k, r in enumerate(text_grads):
        r[...] = dg[k * rows:(k + 1) * rows]
    htxt = mm(ts[...], dg[top], TN)

    @pl.when(first)
    def _():
        other[0:dim] = htxt.astype(BF16)

    @pl.when(jnp.logical_not(first))
    def _():
        keep[0:dim] = htxt

    dg[top] = project(mm(wgt[top], ut[...], NN), pi0, li0)
    dg[low] = project(mm(wgt[low], ut[...], NN), pi1, li1)
    for k, r in ((0, g0), (1, g1), (3, g3)):
        r[0:rows] = dg[k * rows:(k + 1) * rows]
        r[rows:2 * rows] = dg[(k + 4) * rows:(k + 5) * rows]
    g2a[...] = dg[2 * rows:3 * rows]
    g2b[...] = dg[6 * rows:7 * rows]
    himg = mm(xs[...], dg[...], TN)

    @pl.when(first)
    def _():
        keep[0:dim] = himg

    @pl.when(jnp.logical_not(first))
    def _():
        other[0:dim] = himg.astype(BF16)

    mark = split_loss(jnp.full((8, dim), loss, F32), dim)
    keep[dim:dim + 16] = mark.astype(F32)
    other[dim:dim + 16] = mark


def split_loss(total, dim):
    hi = total.astype(BF16)
    lo = (total - hi.astype(F32)).astype(BF16)
    row = lax.broadcasted_iota(jnp.int32, (16, dim), 0)
    return jnp.where(row < 8, jnp.broadcast_to(hi[:1], (16, dim)).astype(F32), jnp.broadcast_to(lo[:1], (16, dim)).astype(F32)).astype(BF16)


def joined_loss(block, start):
    v = block[start:start + 16].astype(F32)
    return v[0:8] + v[8:16]


def core_sum_kernel(part, dim, idx, keep, recv, own, c1, c2, c3, mark):
    me = idx[1]
    at = pl.ds(pl.multiple_of(me * part, part), part)
    own[...] = keep[at] + recv[at].astype(F32)
    total = joined_loss(keep, 4 * part) + joined_loss(recv, 4 * part)
    loss = split_loss(total[:, 0:128], 128)
    mark[...] = loss
    for d, c in enumerate((c1, c2, c3), 1):
        at = pl.ds(pl.multiple_of(lax.rem(me + d, 4) * part, part), part)
        fold(c, (keep[at] + recv[at].astype(F32)).astype(BF16), loss)


def fold(out, block, loss):
    rows, dim = block.shape
    for k in range(dim // 128):
        out[k * rows:(k + 1) * rows] = block[:, k * 128:(k + 1) * 128]
    n = rows * (dim // 128)
    out[n:n + 16] = loss


def unfold(ref, rows, dim):
    n = dim // 128
    return jnp.concatenate([ref[k * rows:(k + 1) * rows].astype(F32) for k in range(n)], axis=1)


def ordered_loss(me, n, slots, mine, others, start):
    slots[me] = mine
    for d, r in others:
        slots[lax.rem(me + n - d, n)] = joined_loss(r, start)
    total = slots[0]
    for k in range(1, n):
        total = total + slots[k]
    return total


def stage_sum_kernel(part, small, dim, idx, own, mark, r1, r2, r3, own2, c1, c2, c3, mark2, full, slots):
    wide = dim // 128
    full[...] = own[...] + (unfold(r1, part, dim) + (unfold(r2, part, dim) + unfold(r3, part, dim)))
    total = ordered_loss(idx[1], 4, slots, joined_loss(mark, 0), ((1, r1), (2, r2), (3, r3)), part * wide)
    loss = split_loss(total, 128)
    mark2[...] = loss
    me = idx[2]
    own2[...] = full[pl.ds(pl.multiple_of(me * small, small), small)]
    for d, c in enumerate((c1, c2, c3), 1):
        at = pl.ds(pl.multiple_of(lax.rem(me + d, 4) * small, small), small)
        fold(c, full[at].astype(BF16), loss)


def second_sum_kernel(small, dim, idx, own, mark, r1, r2, r3, out, slots):
    total = own[...] + (unfold(r1, small, dim) + (unfold(r2, small, dim) + unfold(r3, small, dim)))
    loss = ordered_loss(idx[2], 4, slots, joined_loss(mark, 0), ((1, r1), (2, r2), (3, r3)), small * (dim // 128))
    fold(out, total.astype(BF16), split_loss(loss, 128))


def line_sum_kernel(small, dim, idx, mine, r1, r2, r3, out, parts, slots):
    me = idx[3]
    others = ((1, r1), (2, r2), (3, r3))
    parts[me] = unfold(mine, small, dim)
    for d, r in others:
        parts[lax.rem(me + 4 - d, 4)] = unfold(r, small, dim)
    total = (parts[0] + parts[1]) + (parts[2] + parts[3])
    n = small * (dim // 128)
    loss = ordered_loss(me, 4, slots, joined_loss(mine, n), others, n)
    fold(out, total.astype(BF16), split_loss(loss, 128))


def pair_sum_kernel(small, dim, mine, recv, out, mark):
    out[...] = (unfold(mine, small, dim) + unfold(recv, small, dim)).astype(BF16)
    n = small * (dim // 128)
    loss = joined_loss(mine, n) + joined_loss(recv, n)
    mark[...] = split_loss(jnp.concatenate([loss] * (dim // 128), axis=1), dim)


def quarter_kernel(small, idx, *refs):
    pieces, out = refs[:4], refs[4]
    for d, r in enumerate(pieces):
        out[pl.ds(pl.multiple_of(lax.rem(idx[2] + 4 - d, 4) * small, small), small)] = r[...]


def whole_kernel(part, idx, *refs):
    pieces, mark, out = refs[:4], refs[4], refs[5]
    for d, r in enumerate(pieces):
        out[pl.ds(pl.multiple_of(lax.rem(idx[1] + 4 - d, 4) * part, part), part)] = r[...]
    out[4 * part:4 * part + 16] = mark[...]


def finish_kernel(dim, norm_root, total_rows, idx, mine, theirs, img, txt, loss):
    first = idx[0] == 0
    scale = F32(1.0 / norm_root)

    @pl.when(first)
    def _():
        img[...] = mine[0:dim].astype(F32) * scale
        txt[...] = theirs[0:dim].astype(F32) * scale

    @pl.when(jnp.logical_not(first))
    def _():
        txt[...] = mine[0:dim].astype(F32) * scale
        img[...] = theirs[0:dim].astype(F32) * scale

    both = joined_loss(mine, dim) + joined_loss(theirs, dim)
    loss[0] = jnp.max(both[:, 0:128]) * F32(0.5 / total_rows)


def relay_kernel(rows, g1, g3, from_left, from_right, to_right, to_left):
    to_right[0:rows] = (g1[0:rows].astype(F32) + from_left[...].astype(F32)).astype(BF16)
    to_right[rows:2 * rows] = g1[rows:2 * rows]
    to_left[0:rows] = g3[0:rows]
    to_left[rows:2 * rows] = (g3[rows:2 * rows].astype(F32) + from_right[...].astype(F32)).astype(BF16)


def image_sum_kernel(rows, g0, left, right, own, out):
    total = g0[...].astype(F32) + (left[...].astype(F32) + right[...].astype(F32))
    own[...] = total[0:rows]
    out[...] = total[rows:2 * rows].astype(BF16)


def text_feat_kernel(own, r1, r2, r3, head, out):
    total = (own[...].astype(F32) + r1[...].astype(F32)) + (r2[...].astype(F32) + r3[...].astype(F32))
    out[...] = mm(total.astype(BF16), head[...], NT)


def feat_kernel(own, recv, head, out):
    out[...] = mm((own[...] + recv[...].astype(F32)).astype(BF16), head[...], NT)


def body(img_feat, txt_feat, img_head, txt_head, logit_scale, logit_bias, pair_offset):
    rows, width = img_feat.shape
    dim = img_head.shape[1]
    blk, grp = lax.axis_index("blk"), lax.axis_index("grp")
    core, x, zh = blk % 2, blk // 4, (blk // 2) % 2
    zl, y = grp // 4, grp % 4
    idx = jnp.stack([core, jnp.where(core == 0, x, y), jnp.where(core == 0, y, x), zl]).astype(jnp.int32)
    m = 4 * rows

    h = 2 * rows
    off = pair_offset.reshape(1, rows)
    idx, off, img_feat, txt_feat = after(idx, off, img_feat, txt_feat)
    far = send(img_feat, across_z(1))
    near = [img_feat] + [send(img_feat, along(Y, -d)) for d in (1, 2, 3)]
    later, far, *near = after(txt_feat, far, *near)
    prev_pair = [send(later, along_blk(1)), send(later, across_z(2, along_blk(1)))]
    own_pair = [txt_feat, send(txt_feat, across_z(2))]
    distant = [far] + [send(far, along(Y, -d)) for d in (1, 2, 3)]
    *begun, wi, wt = call(
        lambda *r: first_kernel(rows, *r),
        [
            ((m, width), BF16),
            ((h, width), BF16),
            ((m, dim), F32),
            ((m, dim), BF16),
            ((m, 128), F32),
            ((h, dim), F32),
            ((h, dim), BF16),
            ((h, 128), F32),
            ((m, h), BF16),
            ((8, h), F32),
            ((width, dim), BF16),
            ((width, dim), BF16),
        ],
        2,
        9,
        [pltpu.VMEM((m, h), F32)],
        24,
    )(logit_scale, logit_bias, [near[0]], *near[1:], [own_pair[0]], own_pair[1], [img_head], [txt_head], [off])
    middle = call(
        lambda *r: second_kernel(rows, *r),
        [
            ((h, width), BF16),
            ((h, dim), F32),
            ((h, dim), BF16),
            ((h, 128), F32),
            ((m, h), BF16),
            ((8, h), F32),
        ],
        2,
        5,
        [pltpu.VMEM((m, h), F32)],
    )(logit_scale, logit_bias, begun[3], *prev_pair, wt, [off])

    pair, piece = ((2 * rows, dim), BF16), ((rows, dim), BF16)
    outs = call(
        lambda *r: main_kernel(rows, dim, *r),
        [pair] * 3 + [piece] * 2 + [((dim + 16, dim), F32), ((dim + 16, dim), BF16)] + [piece] * 4,
        3,
        21,
        [
            pltpu.VMEM((2 * m, width), BF16),
            pltpu.VMEM((m, width), BF16),
            pltpu.VMEM((m, dim), F32),
            pltpu.VMEM((2 * m, dim), BF16),
            pltpu.VMEM((m, dim), BF16),
            pltpu.VMEM((m, 128), F32),
            pltpu.VMEM((m, m), F32),
            pltpu.VMEM((2 * m, m), BF16),
            pltpu.VMEM((2 * m, dim), BF16),
            pltpu.VMEM((8, m), F32),
        ],
        32,
    )(idx, logit_scale, logit_bias, *begun, wi, *middle, *distant)
    g0, g1, g3, g2a, g2b, keep, other, own_t, own_far, prev_t, prev_far = outs

    recv = send(other, along(CORE, 1))
    back = [send(prev_t, along_blk(-1)), send(prev_far, across_z(2, along_blk(-1)))]
    part, small, wide = dim // 4, dim // 16, dim // 128
    loss_block = ((16, 128), BF16)
    slots = pltpu.VMEM((4, 8, 128), F32)
    folded = ((small * wide + 16, 128), BF16)
    half = [((rows, dim), F32), ((rows, dim), BF16)]
    own1, a1, a2, a3, mark1 = call(
        lambda *r: core_sum_kernel(part, dim, *r),
        [((part, dim), F32)] + [((part * wide + 16, 128), BF16)] * 3 + [loss_block],
        1,
        2,
    )(idx, keep, recv)
    got = [send(a, by_core(X, Y, d)) for d, a in ((1, a1), (2, a2), (3, a3))]
    own2, b1, b2, b3, mark2 = call(
        lambda *r: stage_sum_kernel(part, small, dim, *r),
        [((small, dim), F32)] + [folded] * 3 + [loss_block],
        1,
        5,
        [pltpu.VMEM((part, dim), F32), slots],
    )(idx, own1, mark1, *got)
    got = [send(b, by_core(Y, X, d)) for d, b in ((1, b1), (2, b2), (3, b3))]
    *got, back[0], back[1] = after(*got, *back)
    (zpart,) = call(lambda *r: second_sum_kernel(small, dim, *r), [folded], 1, 5, [slots])(idx, own2, mark2, *got)
    zpart, g2a, g2b = after(zpart, g2a, g2b)
    got = [send(zpart, along(ZL, d)) for d in (1, 2, 3)]
    from_left, from_right = send(g2a, along(Y, 1)), send(g2b, along(Y, -1))
    (zline,) = call(
        lambda *r: line_sum_kernel(small, dim, *r), [folded], 1, 4, [pltpu.VMEM((4, small, dim), F32), slots]
    )(idx, zpart, *got)
    zline, from_left, from_right = after(zline, from_left, from_right)
    zrecv = send(zline, along(ZH, 1))
    to_right, to_left = call(lambda *r: relay_kernel(rows, *r), [pair] * 2, 0, 4)(g1, g3, from_left, from_right)
    left, right = send(to_right, along(Y, 1)), send(to_left, along(Y, -1))
    done, mark3 = call(
        lambda *r: pair_sum_kernel(small, dim, *r), [((small, dim), BF16), ((16, dim), BF16)], 0, 2
    )(zline, zrecv)
    got = [done] + [send(done, by_core(Y, X, d)) for d in (1, 2, 3)]
    *got, left, right, own_far = after(*got, left, right, own_far)
    img_own, img_out = call(lambda *r: image_sum_kernel(rows, *r), half, 0, 3)(g0, left, right)
    img_in = send(img_out, across_z(1))
    own_in = send(own_far, across_z(2))
    (quarter,) = call(lambda *r: quarter_kernel(small, *r), [((part, dim), BF16)], 1, 4)(idx, *got)
    got = [quarter] + [send(quarter, by_core(X, Y, d)) for d in (1, 2, 3)]
    (whole,) = call(lambda *r: whole_kernel(part, *r), [((dim + 16, dim), BF16)], 1, 5)(idx, *got, mark3)
    whole, img_in, own_in = after(whole, img_in, own_in)
    theirs = send(whole, along(CORE, 1))
    (txt_feat_grad,) = call(text_feat_kernel, [((rows, width), F32)], 0, 5, placed=False)(own_t, own_in, *back, wt)
    (img_feat_grad,) = call(feat_kernel, [((rows, width), F32)], 0, 3, placed=False)(img_own, img_in, wi)
    total_rows = rows * 256
    img_head_grad, txt_head_grad, loss = call(
        lambda *r: finish_kernel(dim, math.sqrt(total_rows), total_rows, *r),
        [((dim, dim), F32)] * 2 + [((1,), F32)],
        1,
        2,
        placed=False,
    )(idx, whole, theirs)

    return img_feat_grad, txt_feat_grad, img_head_grad, txt_head_grad, loss


def solution(mesh):
    rows = P(AXES, None)
    in_specs = (rows, rows, P(), P(), P(), P(), P(AXES))
    out_specs = (rows, rows, P(), P(), P())
    return jax.shard_map(body, mesh=mesh, in_specs=in_specs, out_specs=out_specs, check_vma=False)
```

```python
import math

import jax
import jax.numpy as jnp
from jax import lax
from jax.experimental import pallas as pl
from jax.experimental.pallas import tpu as pltpu
from jax.sharding import PartitionSpec as P

F32 = jnp.float32
BF16 = jnp.bfloat16
NT = (((1,), (1,)), ((), ()))
TN = (((0,), (0,)), ((), ()))
NN = (((1,), (0,)), ((), ()))
AXES = ("blk", "grp")
SIZES = (4, 2, 2, 4, 4)
X, ZH, CORE, ZL, Y = range(5)


def mm(a, b, dims):
    return lax.dot_general(a, b, dims, preferred_element_type=F32)


def coords():
    out = []
    for n in range(256):
        c = []
        for s in reversed(SIZES):
            c.append(n % s)
            n //= s
        out.append(tuple(reversed(c)))
    return out


def index_of(c):
    n = 0
    for s, v in zip(SIZES, c):
        n = n * s + v
    return n


def route(move):
    return [(index_of(c), index_of(move(list(c)))) for c in coords()]


def along(axis, distance):
    def move(c):
        c[axis] = (c[axis] + distance) % SIZES[axis]
        return c

    return route(move)


def by_core(first, second, distance):
    def move(c):
        axis = first if c[CORE] == 0 else second
        c[axis] = (c[axis] + distance) % SIZES[axis]
        return c

    return route(move)


def along_blk(distance):
    return [(i, (i + 16 * distance) % 256) for i in range(256)]


def across_z(bit, pairs=None):
    def move(c):
        c[ZL] = c[ZL] ^ bit
        return c

    turn = dict(route(move))
    return [(i, turn[j]) for i, j in (pairs or [(n, n) for n in range(256)])]


def send(x, pairs):
    return lax.ppermute(x, AXES, pairs)


def after(first, *others):
    return lax.optimization_barrier((first,) + others)


VMEM = pl.BlockSpec(memory_space=pltpu.VMEM)
SMEM = pl.BlockSpec(memory_space=pltpu.SMEM)


def call(kernel, outs, n_smem, n_vmem, scratch=(), limit=16, placed=True):
    def here(shape, dtype):
        if placed and len(shape) > 1:
            return pltpu.VMEM(shape, dtype)
        return jax.ShapeDtypeStruct(shape, dtype)

    run = pl.pallas_call(
        kernel,
        out_shape=[here(s, t) for s, t in outs],
        in_specs=[SMEM] * n_smem + [VMEM] * n_vmem,
        out_specs=[SMEM if len(s) == 1 else VMEM for s, _ in outs],
        scratch_shapes=list(scratch),
        compiler_params=pltpu.CompilerParams(vmem_limit_bytes=limit * 1024 * 1024),
    )

    def launch(*args):
        held = [
            pltpu.with_memory_space_constraint(a[0], pltpu.HBM)
            if isinstance(a, list)
            else pltpu.with_memory_space_constraint(a, pltpu.VMEM)
            for a in args[n_smem:]
        ]
        return run(*args[:n_smem], *held)

    return launch


def lanes(v):
    total = v[:, 0:128]
    for k in range(1, v.shape[1] // 128):
        total = total + v[:, k * 128:(k + 1) * 128]
    return jnp.sum(total, axis=-1, keepdims=True)


def normalise(proj, direction, unit, inv, at):
    s = lax.rsqrt(lanes(proj * proj) + 1e-06)
    d = proj * s
    direction[...] = d
    unit[at] = d.astype(BF16)
    inv[...] = jnp.broadcast_to(s, inv.shape)


def project(g, direction, inv):
    d = direction[...]
    s = inv[...][:, :1]
    inner = lanes(d * g)
    return (g * s - d * (inner * s)).astype(BF16)


def score(lg, wgt, acc, scal, down, right, marked=0, which=None, flat=False):
    n, columns = lg.shape
    temper, bias = scal[0][0], scal[1][0]
    if marked:
        off, here_set = which
        wanted = jnp.concatenate([off[...], jnp.full((1, columns - marked), -1, jnp.int32)], axis=1) == here_set

    def step(i, masked):
        here = (pl.ds(i * 64, 64) if isinstance(i, int) else pl.ds(pl.multiple_of(i * 64, 64), 64))
        l = temper * lg[here] + bias
        t = 64.0 * temper
        if masked:
            row = lax.broadcasted_iota(jnp.int32, (64, columns), 0) + i * 64
            col = lax.broadcasted_iota(jnp.int32, (64, columns), 1)
            pos = (col == row) & wanted
            l = jnp.where(pos, -l, l)
            t = jnp.where(pos, -t, t)
        e = jnp.exp(l)
        u = 1.0 + e
        r = 1.0 / u
        terms = jnp.log(u) + (e - (u - 1.0)) * r
        total = terms[0:8]
        for k in range(1, 8):
            total = total + terms[k * 8:(k + 1) * 8]
        acc[:, 0:columns] += total
        there = pl.ds(down + i * 64, 64) if isinstance(i, int) else pl.ds(pl.multiple_of(down + i * 64, 64), 64)
        wgt[there, right:right + columns] = (t * (e * r)).astype(BF16)
        return 0

    if marked and flat:
        for i in range(marked // 64):
            step(i, True)
    elif marked:
        lax.fori_loop(0, marked // 64, lambda i, _: step(i, True), 0)
    if flat:
        for i in range(marked // 64, n // 64):
            step(i, False)
    else:
        lax.fori_loop(marked // 64, n // 64, lambda i, _: step(i, False), 0)


def first_kernel(rows, temper, bias, x0, x1, x2, x3, t0, t1, wi, wt, off, *refs):
    xs, ts, pi, ui, li, pt, ut, lt, wgt, acc, wi_out, wt_out, lg = refs
    for k, r in enumerate((x0, x1, x2, x3)):
        xs[k * rows:(k + 1) * rows] = r[...]
    for k, r in enumerate((t0, t1)):
        ts[k * rows:(k + 1) * rows] = r[...]
    wi_out[...] = wi[...]
    wt_out[...] = wt[...]
    normalise(mm(ts[...], wt[...], NN), pt, ut, lt, slice(None))
    normalise(mm(xs[...], wi[...], NN), pi, ui, li, slice(None))
    lg[...] = mm(ui[...], ut[...], NT)
    acc[...] = jnp.zeros_like(acc)
    score(lg, wgt, acc, (temper, bias), 0, 0, rows, (off, 0))


def second_kernel(rows, temper, bias, ui, t0, t1, wt, off, ts, pt, ut, lt, wgt, acc, lg):
    for k, r in enumerate((t0, t1)):
        ts[k * rows:(k + 1) * rows] = r[...]
    normalise(mm(ts[...], wt[...], NN), pt, ut, lt, slice(None))
    lg[...] = mm(ui[...], ut[...], NT)
    acc[...] = jnp.zeros_like(acc)
    score(lg, wgt, acc, (temper, bias), 0, 0, rows, (off, 1), flat=True)


def main_kernel(rows, dim, *refs):
    idx, scal, (xs0, ts0, pi0, ui0, li0, pt0, ut0, lt0, wgt0, acc0, wi) = refs[0], refs[1:3], refs[3:14]
    (ts1, pt1, ut1, lt1, wgt1, acc1), images = refs[14:20], refs[20:24]
    g0, g1, g3, g2a, g2b, keep, other = refs[24:31]
    text_grads = refs[31:35]
    xs, ts, pi1, ui, ut, li1, lg, wgt, dg, dt, acc = refs[35:]
    m, h = 4 * rows, 2 * rows
    top, low = slice(0, m), slice(m, 2 * m)
    front, rear = slice(0, h), slice(h, m)
    xs[top] = xs0[...]
    ui[top] = ui0[...]
    ts[front] = ts0[...]
    ts[rear] = ts1[...]
    ut[front] = ut0[...]
    ut[rear] = ut1[...]
    wgt[top, 0:h] = wgt0[...]
    wgt[top, h:m] = wgt1[...]
    acc[:, 0:h] = acc0[...]
    acc[:, h:m] = acc1[...]
    for k, r in enumerate(images):
        xs[m + k * rows:m + (k + 1) * rows] = r[...]

    proj = mm(xs[low], wi[...], NN)
    part_top = mm(wgt[top], ut[...], NN)
    normalise(proj, pi1, ui, li1, low)
    lg[...] = mm(ui[low], ut[...], NT)
    upper = mm(wgt[top], ui[top], TN)
    dg[top] = project(part_top, pi0, li0)
    score(lg, wgt, acc, scal, m, 0, flat=True)
    part_low = mm(wgt[low], ut[...], NN)
    grad = upper + mm(wgt[low], ui[low], TN)
    dt[front] = project(grad[front], pt0, lt0)
    dt[rear] = project(grad[rear], pt1, lt1)
    dg[low] = project(part_low, pi1, li1)
    loss = jnp.sum(acc[...])

    first = idx[0] == 0
    for k, r in enumerate(text_grads):
        r[...] = dt[k * rows:(k + 1) * rows]
    for k, r in ((0, g0), (1, g1), (3, g3)):
        r[0:rows] = dg[k * rows:(k + 1) * rows]
        r[rows:2 * rows] = dg[(k + 4) * rows:(k + 5) * rows]
    g2a[...] = dg[2 * rows:3 * rows]
    g2b[...] = dg[6 * rows:7 * rows]
    htxt = mm(ts[...], dt[...], TN)
    himg = mm(xs[...], dg[...], TN)

    @pl.when(first)
    def _():
        keep[0:dim] = himg
        other[0:dim] = htxt.astype(BF16)

    @pl.when(jnp.logical_not(first))
    def _():
        keep[0:dim] = htxt
        other[0:dim] = himg.astype(BF16)

    mark = split_loss(jnp.full((8, dim), loss, F32), dim)
    keep[dim:dim + 16] = mark.astype(F32)
    other[dim:dim + 16] = mark


def split_loss(total, dim):
    hi = total.astype(BF16)
    lo = (total - hi.astype(F32)).astype(BF16)
    row = lax.broadcasted_iota(jnp.int32, (16, dim), 0)
    return jnp.where(row < 8, jnp.broadcast_to(hi[:1], (16, dim)).astype(F32), jnp.broadcast_to(lo[:1], (16, dim)).astype(F32)).astype(BF16)


def joined_loss(block, start):
    v = block[start:start + 16].astype(F32)
    return v[0:8] + v[8:16]


def core_sum_kernel(part, dim, idx, keep, recv, own, c1, c2, c3, mark):
    me = idx[1]
    at = pl.ds(pl.multiple_of(me * part, part), part)
    own[...] = keep[at] + recv[at].astype(F32)
    total = joined_loss(keep, 4 * part) + joined_loss(recv, 4 * part)
    loss = split_loss(total[:, 0:128], 128)
    mark[...] = loss
    for d, c in enumerate((c1, c2, c3), 1):
        at = pl.ds(pl.multiple_of(lax.rem(me + d, 4) * part, part), part)
        fold(c, (keep[at] + recv[at].astype(F32)).astype(BF16), loss)


def fold(out, block, loss):
    rows, dim = block.shape
    for k in range(dim // 128):
        out[k * rows:(k + 1) * rows] = block[:, k * 128:(k + 1) * 128]
    n = rows * (dim // 128)
    out[n:n + 16] = loss


def unfold(ref, rows, dim):
    n = dim // 128
    return jnp.concatenate([ref[k * rows:(k + 1) * rows].astype(F32) for k in range(n)], axis=1)


def ordered_loss(me, n, slots, mine, others, start):
    slots[me] = mine
    for d, r in others:
        slots[lax.rem(me + n - d, n)] = joined_loss(r, start)
    total = slots[0]
    for k in range(1, n):
        total = total + slots[k]
    return total


def stage_sum_kernel(part, small, dim, idx, own, mark, r1, r2, r3, own2, c1, c2, c3, mark2, full, slots):
    wide = dim // 128
    full[...] = own[...] + (unfold(r1, part, dim) + (unfold(r2, part, dim) + unfold(r3, part, dim)))
    total = ordered_loss(idx[1], 4, slots, joined_loss(mark, 0), ((1, r1), (2, r2), (3, r3)), part * wide)
    loss = split_loss(total, 128)
    mark2[...] = loss
    me = idx[2]
    own2[...] = full[pl.ds(pl.multiple_of(me * small, small), small)]
    for d, c in enumerate((c1, c2, c3), 1):
        at = pl.ds(pl.multiple_of(lax.rem(me + d, 4) * small, small), small)
        fold(c, full[at].astype(BF16), loss)


def second_sum_kernel(small, dim, idx, own, mark, r1, r2, r3, out, slots):
    total = own[...] + (unfold(r1, small, dim) + (unfold(r2, small, dim) + unfold(r3, small, dim)))
    loss = ordered_loss(idx[2], 4, slots, joined_loss(mark, 0), ((1, r1), (2, r2), (3, r3)), small * (dim // 128))
    fold(out, total.astype(BF16), split_loss(loss, 128))


def line_sum_kernel(small, dim, idx, mine, r1, r2, r3, out, parts, slots):
    me = idx[3]
    others = ((1, r1), (2, r2), (3, r3))
    parts[me] = unfold(mine, small, dim)
    for d, r in others:
        parts[lax.rem(me + 4 - d, 4)] = unfold(r, small, dim)
    total = (parts[0] + parts[1]) + (parts[2] + parts[3])
    n = small * (dim // 128)
    loss = ordered_loss(me, 4, slots, joined_loss(mine, n), others, n)
    fold(out, total.astype(BF16), split_loss(loss, 128))


def pair_sum_kernel(small, dim, mine, recv, out, mark):
    out[...] = (unfold(mine, small, dim) + unfold(recv, small, dim)).astype(BF16)
    n = small * (dim // 128)
    loss = joined_loss(mine, n) + joined_loss(recv, n)
    mark[...] = split_loss(jnp.concatenate([loss] * (dim // 128), axis=1), dim)


def quarter_kernel(small, idx, *refs):
    pieces, out = refs[:4], refs[4]
    for d, r in enumerate(pieces):
        out[pl.ds(pl.multiple_of(lax.rem(idx[2] + 4 - d, 4) * small, small), small)] = r[...]


def whole_kernel(part, idx, *refs):
    pieces, mark, out = refs[:4], refs[4], refs[5]
    for d, r in enumerate(pieces):
        out[pl.ds(pl.multiple_of(lax.rem(idx[1] + 4 - d, 4) * part, part), part)] = r[...]
    out[4 * part:4 * part + 16] = mark[...]


def finish_kernel(dim, norm_root, total_rows, idx, mine, theirs, img, txt, loss):
    first = idx[0] == 0
    scale = F32(1.0 / norm_root)

    @pl.when(first)
    def _():
        img[...] = mine[0:dim].astype(F32) * scale
        txt[...] = theirs[0:dim].astype(F32) * scale

    @pl.when(jnp.logical_not(first))
    def _():
        txt[...] = mine[0:dim].astype(F32) * scale
        img[...] = theirs[0:dim].astype(F32) * scale

    both = joined_loss(mine, dim) + joined_loss(theirs, dim)
    loss[0] = jnp.max(both[:, 0:128]) * F32(0.5 / total_rows)


def relay_kernel(rows, g1, g3, from_left, from_right, to_right, to_left):
    to_right[0:rows] = (g1[0:rows].astype(F32) + from_left[...].astype(F32)).astype(BF16)
    to_right[rows:2 * rows] = g1[rows:2 * rows]
    to_left[0:rows] = g3[0:rows]
    to_left[rows:2 * rows] = (g3[rows:2 * rows].astype(F32) + from_right[...].astype(F32)).astype(BF16)


def image_sum_kernel(rows, g0, left, right, own, out):
    total = g0[...].astype(F32) + (left[...].astype(F32) + right[...].astype(F32))
    own[...] = total[0:rows]
    out[...] = total[rows:2 * rows].astype(BF16)


def text_feat_kernel(own, r1, r2, r3, head, out):
    total = (own[...].astype(F32) + r1[...].astype(F32)) + (r2[...].astype(F32) + r3[...].astype(F32))
    out[...] = mm(total.astype(BF16), head[...], NT)


def feat_kernel(own, recv, head, out):
    out[...] = mm((own[...] + recv[...].astype(F32)).astype(BF16), head[...], NT)


def body(img_feat, txt_feat, img_head, txt_head, logit_scale, logit_bias, pair_offset):
    rows, width = img_feat.shape
    dim = img_head.shape[1]
    blk, grp = lax.axis_index("blk"), lax.axis_index("grp")
    core, x, zh = blk % 2, blk // 4, (blk // 2) % 2
    zl, y = grp // 4, grp % 4
    idx = jnp.stack([core, jnp.where(core == 0, x, y), jnp.where(core == 0, y, x), zl]).astype(jnp.int32)
    m = 4 * rows

    h = 2 * rows
    off = pair_offset.reshape(1, rows)
    idx, off, img_feat, txt_feat = after(idx, off, img_feat, txt_feat)
    far = send(img_feat, across_z(1))
    near = [img_feat] + [send(img_feat, along(Y, -d)) for d in (1, 2, 3)]
    later, far, *near = after(txt_feat, far, *near)
    prev_pair = [send(later, along_blk(1)), send(later, across_z(2, along_blk(1)))]
    own_pair = [txt_feat, send(txt_feat, across_z(2))]
    distant = [far] + [send(far, along(Y, -d)) for d in (1, 2, 3)]
    *begun, wi, wt = call(
        lambda *r: first_kernel(rows, *r),
        [
            ((m, width), BF16),
            ((h, width), BF16),
            ((m, dim), F32),
            ((m, dim), BF16),
            ((m, 128), F32),
            ((h, dim), F32),
            ((h, dim), BF16),
            ((h, 128), F32),
            ((m, h), BF16),
            ((8, h), F32),
            ((width, dim), BF16),
            ((width, dim), BF16),
        ],
        2,
        9,
        [pltpu.VMEM((m, h), F32)],
        24,
    )(logit_scale, logit_bias, [near[0]], *near[1:], [own_pair[0]], own_pair[1], [img_head], [txt_head], [off])
    middle = call(
        lambda *r: second_kernel(rows, *r),
        [
            ((h, width), BF16),
            ((h, dim), F32),
            ((h, dim), BF16),
            ((h, 128), F32),
            ((m, h), BF16),
            ((8, h), F32),
        ],
        2,
        5,
        [pltpu.VMEM((m, h), F32)],
    )(logit_scale, logit_bias, begun[3], *prev_pair, wt, [off])

    pair, piece = ((2 * rows, dim), BF16), ((rows, dim), BF16)
    outs = call(
        lambda *r: main_kernel(rows, dim, *r),
        [pair] * 3 + [piece] * 2 + [((dim + 16, dim), F32), ((dim + 16, dim), BF16)] + [piece] * 4,
        3,
        21,
        [
            pltpu.VMEM((2 * m, width), BF16),
            pltpu.VMEM((m, width), BF16),
            pltpu.VMEM((m, dim), F32),
            pltpu.VMEM((2 * m, dim), BF16),
            pltpu.VMEM((m, dim), BF16),
            pltpu.VMEM((m, 128), F32),
            pltpu.VMEM((m, m), F32),
            pltpu.VMEM((2 * m, m), BF16),
            pltpu.VMEM((2 * m, dim), BF16),
            pltpu.VMEM((m, dim), BF16),
            pltpu.VMEM((8, m), F32),
        ],
        34,
    )(idx, logit_scale, logit_bias, *begun, wi, *middle, *distant)
    g0, g1, g3, g2a, g2b, keep, other, own_t, own_far, prev_t, prev_far = outs

    recv = send(other, along(CORE, 1))
    back = [send(prev_t, along_blk(-1)), send(prev_far, across_z(2, along_blk(-1)))]
    part, small, wide = dim // 4, dim // 16, dim // 128
    loss_block = ((16, 128), BF16)
    slots = pltpu.VMEM((4, 8, 128), F32)
    folded = ((small * wide + 16, 128), BF16)
    half = [((rows, dim), F32), ((rows, dim), BF16)]
    own1, a1, a2, a3, mark1 = call(
        lambda *r: core_sum_kernel(part, dim, *r),
        [((part, dim), F32)] + [((part * wide + 16, 128), BF16)] * 3 + [loss_block],
        1,
        2,
    )(idx, keep, recv)
    got = [send(a, by_core(X, Y, d)) for d, a in ((1, a1), (2, a2), (3, a3))]
    own2, b1, b2, b3, mark2 = call(
        lambda *r: stage_sum_kernel(part, small, dim, *r),
        [((small, dim), F32)] + [folded] * 3 + [loss_block],
        1,
        5,
        [pltpu.VMEM((part, dim), F32), slots],
    )(idx, own1, mark1, *got)
    got = [send(b, by_core(Y, X, d)) for d, b in ((1, b1), (2, b2), (3, b3))]
    *got, back[0], back[1] = after(*got, *back)
    (zpart,) = call(lambda *r: second_sum_kernel(small, dim, *r), [folded], 1, 5, [slots])(idx, own2, mark2, *got)
    zpart, g2a, g2b = after(zpart, g2a, g2b)
    got = [send(zpart, along(ZL, d)) for d in (1, 2, 3)]
    from_left, from_right = send(g2a, along(Y, 1)), send(g2b, along(Y, -1))
    (zline,) = call(
        lambda *r: line_sum_kernel(small, dim, *r), [folded], 1, 4, [pltpu.VMEM((4, small, dim), F32), slots]
    )(idx, zpart, *got)
    zline, from_left, from_right = after(zline, from_left, from_right)
    zrecv = send(zline, along(ZH, 1))
    to_right, to_left = call(lambda *r: relay_kernel(rows, *r), [pair] * 2, 0, 4)(g1, g3, from_left, from_right)
    left, right = send(to_right, along(Y, 1)), send(to_left, along(Y, -1))
    done, mark3 = call(
        lambda *r: pair_sum_kernel(small, dim, *r), [((small, dim), BF16), ((16, dim), BF16)], 0, 2
    )(zline, zrecv)
    got = [done] + [send(done, by_core(Y, X, d)) for d in (1, 2, 3)]
    *got, left, right, own_far = after(*got, left, right, own_far)
    img_own, img_out = call(lambda *r: image_sum_kernel(rows, *r), half, 0, 3)(g0, left, right)
    img_in = send(img_out, across_z(1))
    own_in = send(own_far, across_z(2))
    (quarter,) = call(lambda *r: quarter_kernel(small, *r), [((part, dim), BF16)], 1, 4)(idx, *got)
    got = [quarter] + [send(quarter, by_core(X, Y, d)) for d in (1, 2, 3)]
    (whole,) = call(lambda *r: whole_kernel(part, *r), [((dim + 16, dim), BF16)], 1, 5)(idx, *got, mark3)
    whole, img_in, own_in = after(whole, img_in, own_in)
    theirs = send(whole, along(CORE, 1))
    (txt_feat_grad,) = call(text_feat_kernel, [((rows, width), F32)], 0, 5, placed=False)(own_t, own_in, *back, wt)
    (img_feat_grad,) = call(feat_kernel, [((rows, width), F32)], 0, 3, placed=False)(img_own, img_in, wi)
    total_rows = rows * 256
    img_head_grad, txt_head_grad, loss = call(
        lambda *r: finish_kernel(dim, math.sqrt(total_rows), total_rows, *r),
        [((dim, dim), F32)] * 2 + [((1,), F32)],
        1,
        2,
        placed=False,
    )(idx, whole, theirs)

    return img_feat_grad, txt_feat_grad, img_head_grad, txt_head_grad, loss


def solution(mesh):
    rows = P(AXES, None)
    in_specs = (rows, rows, P(), P(), P(), P(), P(AXES))
    out_specs = (rows, rows, P(), P(), P())
    return jax.shard_map(body, mesh=mesh, in_specs=in_specs, out_specs=out_specs, check_vma=False)
```

```python
import math

import jax
import jax.numpy as jnp
from jax import lax
from jax.experimental import pallas as pl
from jax.experimental.pallas import tpu as pltpu
from jax.sharding import PartitionSpec as P

F32 = jnp.float32
BF16 = jnp.bfloat16
NT = (((1,), (1,)), ((), ()))
TN = (((0,), (0,)), ((), ()))
NN = (((1,), (0,)), ((), ()))
AXES = ("blk", "grp")
SIZES = (4, 2, 2, 4, 4)
X, ZH, CORE, ZL, Y = range(5)


def mm(a, b, dims):
    return lax.dot_general(a, b, dims, preferred_element_type=F32)


def coords():
    out = []
    for n in range(256):
        c = []
        for s in reversed(SIZES):
            c.append(n % s)
            n //= s
        out.append(tuple(reversed(c)))
    return out


def index_of(c):
    n = 0
    for s, v in zip(SIZES, c):
        n = n * s + v
    return n


def route(move):
    return [(index_of(c), index_of(move(list(c)))) for c in coords()]


def along(axis, distance):
    def move(c):
        c[axis] = (c[axis] + distance) % SIZES[axis]
        return c

    return route(move)


def by_core(first, second, distance):
    def move(c):
        axis = first if c[CORE] == 0 else second
        c[axis] = (c[axis] + distance) % SIZES[axis]
        return c

    return route(move)


def along_blk(distance):
    return [(i, (i + 16 * distance) % 256) for i in range(256)]


def across_z(bit, pairs=None):
    def move(c):
        c[ZL] = c[ZL] ^ bit
        return c

    turn = dict(route(move))
    return [(i, turn[j]) for i, j in (pairs or [(n, n) for n in range(256)])]


def send(x, pairs):
    return lax.ppermute(x, AXES, pairs)


def after(first, *others):
    return lax.optimization_barrier((first,) + others)


VMEM = pl.BlockSpec(memory_space=pltpu.VMEM)
SMEM = pl.BlockSpec(memory_space=pltpu.SMEM)


def call(kernel, outs, n_smem, n_vmem, scratch=(), limit=16, placed=True):
    def here(shape, dtype):
        if placed and len(shape) > 1:
            return pltpu.VMEM(shape, dtype)
        return jax.ShapeDtypeStruct(shape, dtype)

    run = pl.pallas_call(
        kernel,
        out_shape=[here(s, t) for s, t in outs],
        in_specs=[SMEM] * n_smem + [VMEM] * n_vmem,
        out_specs=[SMEM if len(s) == 1 else VMEM for s, _ in outs],
        scratch_shapes=list(scratch),
        compiler_params=pltpu.CompilerParams(vmem_limit_bytes=limit * 1024 * 1024),
    )

    def launch(*args):
        held = [
            pltpu.with_memory_space_constraint(a[0], pltpu.HBM)
            if isinstance(a, list)
            else pltpu.with_memory_space_constraint(a, pltpu.VMEM)
            for a in args[n_smem:]
        ]
        return run(*args[:n_smem], *held)

    return launch


def lanes(v):
    total = v[:, 0:128]
    for k in range(1, v.shape[1] // 128):
        total = total + v[:, k * 128:(k + 1) * 128]
    return jnp.sum(total, axis=-1, keepdims=True)


def normalise(proj, direction, unit, inv, at):
    s = lax.rsqrt(lanes(proj * proj) + 1e-06)
    d = proj * s
    direction[...] = d
    unit[at] = d.astype(BF16)
    inv[...] = jnp.broadcast_to(s, inv.shape)


def project(g, direction, inv):
    d = direction[...]
    s = inv[...][:, :1]
    inner = lanes(d * g)
    return (g * s - d * (inner * s)).astype(BF16)


def score(lg, wgt, acc, scal, down, right, marked=0, which=None, flat=False):
    n, columns = lg.shape
    temper, bias = scal[0][0], scal[1][0]
    if marked:
        off, here_set = which
        wanted = jnp.concatenate([off[...], jnp.full((1, columns - marked), -1, jnp.int32)], axis=1) == here_set

    def step(i, masked):
        here = (pl.ds(i * 64, 64) if isinstance(i, int) else pl.ds(pl.multiple_of(i * 64, 64), 64))
        l = temper * lg[here] + bias
        t = 64.0 * temper
        if masked:
            row = lax.broadcasted_iota(jnp.int32, (64, columns), 0) + i * 64
            col = lax.broadcasted_iota(jnp.int32, (64, columns), 1)
            pos = (col == row) & wanted
            l = jnp.where(pos, -l, l)
            t = jnp.where(pos, -t, t)
        e = jnp.exp(l)
        u = 1.0 + e
        r = 1.0 / u
        terms = jnp.log(u) + (e - (u - 1.0)) * r
        total = terms[0:8]
        for k in range(1, 8):
            total = total + terms[k * 8:(k + 1) * 8]
        acc[:, 0:columns] += total
        there = pl.ds(down + i * 64, 64) if isinstance(i, int) else pl.ds(pl.multiple_of(down + i * 64, 64), 64)
        wgt[there, right:right + columns] = (t * (e * r)).astype(BF16)
        return 0

    if marked and flat:
        for i in range(marked // 64):
            step(i, True)
    elif marked:
        lax.fori_loop(0, marked // 64, lambda i, _: step(i, True), 0)
    if flat:
        for i in range(marked // 64, n // 64):
            step(i, False)
    else:
        lax.fori_loop(marked // 64, n // 64, lambda i, _: step(i, False), 0)


def first_kernel(rows, temper, bias, x0, x1, x2, x3, t0, t1, wi, wt, off, *refs):
    xs, ts, pi, ui, li, pt, ut, lt, wgt, acc, wi_out, wt_out, lg = refs
    for k, r in enumerate((x0, x1, x2, x3)):
        xs[k * rows:(k + 1) * rows] = r[...]
    for k, r in enumerate((t0, t1)):
        ts[k * rows:(k + 1) * rows] = r[...]
    wi_out[...] = wi[...]
    wt_out[...] = wt[...]
    normalise(mm(ts[...], wt[...], NN), pt, ut, lt, slice(None))
    normalise(mm(xs[...], wi[...], NN), pi, ui, li, slice(None))
    lg[...] = mm(ui[...], ut[...], NT)
    acc[...] = jnp.zeros_like(acc)
    score(lg, wgt, acc, (temper, bias), 0, 0, rows, (off, 0))


def second_kernel(rows, temper, bias, ui, t0, t1, wt, off, ts, pt, ut, lt, wgt, acc, lg):
    for k, r in enumerate((t0, t1)):
        ts[k * rows:(k + 1) * rows] = r[...]
    normalise(mm(ts[...], wt[...], NN), pt, ut, lt, slice(None))
    lg[...] = mm(ui[...], ut[...], NT)
    acc[...] = jnp.zeros_like(acc)
    score(lg, wgt, acc, (temper, bias), 0, 0, rows, (off, 1), flat=True)


def main_kernel(rows, dim, *refs):
    idx, scal, (xs0, ts0, pi0, ui0, li0, pt0, ut0, lt0, wgt0, acc0, wi) = refs[0], refs[1:3], refs[3:14]
    (ts1, pt1, ut1, lt1, wgt1, acc1), images = refs[14:20], refs[20:24]
    g0, g1, g3, g2a, g2b, keep, other = refs[24:31]
    text_grads = refs[31:35]
    xs, ts, pi1, ui, ut, li1, lg, wgt, dg, dt, acc = refs[35:]
    m, h = 4 * rows, 2 * rows
    top, low = slice(0, m), slice(m, 2 * m)
    front, rear = slice(0, h), slice(h, m)
    xs[top] = xs0[...]
    ui[top] = ui0[...]
    ts[front] = ts0[...]
    ts[rear] = ts1[...]
    ut[front] = ut0[...]
    ut[rear] = ut1[...]
    wgt[top, 0:h] = wgt0[...]
    wgt[top, h:m] = wgt1[...]
    acc[:, 0:h] = acc0[...]
    acc[:, h:m] = acc1[...]
    for k, r in enumerate(images):
        xs[m + k * rows:m + (k + 1) * rows] = r[...]

    proj = mm(xs[low], wi[...], NN)
    part_top = mm(wgt[top], ut[...], NN)
    normalise(proj, pi1, ui, li1, low)
    lg[...] = mm(ui[low], ut[...], NT)
    upper = mm(wgt[top], ui[top], TN)
    dg[top] = project(part_top, pi0, li0)
    score(lg, wgt, acc, scal, m, 0, flat=True)
    part_low = mm(wgt[low], ut[...], NN)
    grad = upper + mm(wgt[low], ui[low], TN)
    dt[front] = project(grad[front], pt0, lt0)
    dt[rear] = project(grad[rear], pt1, lt1)
    dg[low] = project(part_low, pi1, li1)
    loss = jnp.sum(acc[...])

    first = idx[0] == 0
    for k, r in enumerate(text_grads):
        r[...] = dt[k * rows:(k + 1) * rows]
    for k, r in ((0, g0), (1, g1), (3, g3)):
        r[0:rows] = dg[k * rows:(k + 1) * rows]
        r[rows:2 * rows] = dg[(k + 4) * rows:(k + 5) * rows]
    g2a[...] = dg[2 * rows:3 * rows]
    g2b[...] = dg[6 * rows:7 * rows]
    htxt = mm(ts[...], dt[...], TN)
    himg = mm(xs[...], dg[...], TN)

    @pl.when(first)
    def _():
        keep[0:dim] = himg
        other[0:dim] = htxt.astype(BF16)

    @pl.when(jnp.logical_not(first))
    def _():
        keep[0:dim] = htxt
        other[0:dim] = himg.astype(BF16)

    mark = split_loss(jnp.full((8, dim), loss, F32), dim)
    keep[dim:dim + 16] = mark.astype(F32)
    other[dim:dim + 16] = mark


def split_loss(total, dim):
    hi = total.astype(BF16)
    lo = (total - hi.astype(F32)).astype(BF16)
    row = lax.broadcasted_iota(jnp.int32, (16, dim), 0)
    return jnp.where(row < 8, jnp.broadcast_to(hi[:1], (16, dim)).astype(F32), jnp.broadcast_to(lo[:1], (16, dim)).astype(F32)).astype(BF16)


def joined_loss(block, start):
    v = block[start:start + 16].astype(F32)
    return v[0:8] + v[8:16]


def core_sum_kernel(part, dim, idx, keep, recv, own, c1, c2, c3, mark):
    me = idx[1]
    at = pl.ds(pl.multiple_of(me * part, part), part)
    own[...] = keep[at] + recv[at].astype(F32)
    total = joined_loss(keep, 4 * part) + joined_loss(recv, 4 * part)
    loss = split_loss(total[:, 0:128], 128)
    mark[...] = loss
    for d, c in enumerate((c1, c2, c3), 1):
        at = pl.ds(pl.multiple_of(lax.rem(me + d, 4) * part, part), part)
        fold(c, (keep[at] + recv[at].astype(F32)).astype(BF16), loss)


def fold(out, block, loss):
    rows, dim = block.shape
    for k in range(dim // 128):
        out[k * rows:(k + 1) * rows] = block[:, k * 128:(k + 1) * 128]
    n = rows * (dim // 128)
    out[n:n + 16] = loss


def unfold(ref, rows, dim):
    n = dim // 128
    return jnp.concatenate([ref[k * rows:(k + 1) * rows].astype(F32) for k in range(n)], axis=1)


def ordered_loss(me, n, slots, mine, others, start):
    slots[me] = mine
    for d, r in others:
        slots[lax.rem(me + n - d, n)] = joined_loss(r, start)
    total = slots[0]
    for k in range(1, n):
        total = total + slots[k]
    return total


def stage_sum_kernel(part, small, dim, idx, own, mark, r1, r2, r3, own2, c1, c2, c3, mark2, full, slots):
    wide = dim // 128
    full[...] = own[...] + (unfold(r1, part, dim) + (unfold(r2, part, dim) + unfold(r3, part, dim)))
    total = ordered_loss(idx[1], 4, slots, joined_loss(mark, 0), ((1, r1), (2, r2), (3, r3)), part * wide)
    loss = split_loss(total, 128)
    mark2[...] = loss
    me = idx[2]
    own2[...] = full[pl.ds(pl.multiple_of(me * small, small), small)]
    for d, c in enumerate((c1, c2, c3), 1):
        at = pl.ds(pl.multiple_of(lax.rem(me + d, 4) * small, small), small)
        fold(c, full[at].astype(BF16), loss)


def second_sum_kernel(small, dim, idx, own, mark, r1, r2, r3, out, slots):
    total = own[...] + (unfold(r1, small, dim) + (unfold(r2, small, dim) + unfold(r3, small, dim)))
    loss = ordered_loss(idx[2], 4, slots, joined_loss(mark, 0), ((1, r1), (2, r2), (3, r3)), small * (dim // 128))
    fold(out, total.astype(BF16), split_loss(loss, 128))


def line_sum_kernel(small, dim, idx, mine, r1, r2, r3, out, parts, slots):
    me = idx[3]
    others = ((1, r1), (2, r2), (3, r3))
    parts[me] = unfold(mine, small, dim)
    for d, r in others:
        parts[lax.rem(me + 4 - d, 4)] = unfold(r, small, dim)
    total = (parts[0] + parts[1]) + (parts[2] + parts[3])
    n = small * (dim // 128)
    loss = ordered_loss(me, 4, slots, joined_loss(mine, n), others, n)
    fold(out, total.astype(BF16), split_loss(loss, 128))


def pair_sum_kernel(small, dim, mine, recv, out, mark):
    out[...] = (unfold(mine, small, dim) + unfold(recv, small, dim)).astype(BF16)
    n = small * (dim // 128)
    loss = joined_loss(mine, n) + joined_loss(recv, n)
    mark[...] = split_loss(jnp.concatenate([loss] * (dim // 128), axis=1), dim)


def quarter_kernel(small, idx, *refs):
    pieces, out = refs[:4], refs[4]
    for d, r in enumerate(pieces):
        out[pl.ds(pl.multiple_of(lax.rem(idx[2] + 4 - d, 4) * small, small), small)] = r[...]


def whole_kernel(part, idx, *refs):
    pieces, mark, out = refs[:4], refs[4], refs[5]
    for d, r in enumerate(pieces):
        out[pl.ds(pl.multiple_of(lax.rem(idx[1] + 4 - d, 4) * part, part), part)] = r[...]
    out[4 * part:4 * part + 16] = mark[...]


def finish_kernel(dim, norm_root, total_rows, idx, mine, theirs, img, txt, loss):
    first = idx[0] == 0
    scale = F32(1.0 / norm_root)

    @pl.when(first)
    def _():
        img[...] = mine[0:dim].astype(F32) * scale
        txt[...] = theirs[0:dim].astype(F32) * scale

    @pl.when(jnp.logical_not(first))
    def _():
        txt[...] = mine[0:dim].astype(F32) * scale
        img[...] = theirs[0:dim].astype(F32) * scale

    both = joined_loss(mine, dim) + joined_loss(theirs, dim)
    loss[0] = jnp.max(both[:, 0:128]) * F32(0.5 / total_rows)


def relay_kernel(rows, g1, g3, from_left, from_right, to_right, to_left):
    to_right[0:rows] = (g1[0:rows].astype(F32) + from_left[...].astype(F32)).astype(BF16)
    to_right[rows:2 * rows] = g1[rows:2 * rows]
    to_left[0:rows] = g3[0:rows]
    to_left[rows:2 * rows] = (g3[rows:2 * rows].astype(F32) + from_right[...].astype(F32)).astype(BF16)


def image_sum_kernel(rows, g0, left, right, own, out):
    total = g0[...].astype(F32) + (left[...].astype(F32) + right[...].astype(F32))
    own[...] = total[0:rows]
    out[...] = total[rows:2 * rows].astype(BF16)


def text_feat_kernel(own, r1, r2, r3, head, out):
    total = (own[...].astype(F32) + r1[...].astype(F32)) + (r2[...].astype(F32) + r3[...].astype(F32))
    out[...] = mm(total.astype(BF16), head[...], NT)


def feat_kernel(own, recv, head, out):
    out[...] = mm((own[...] + recv[...].astype(F32)).astype(BF16), head[...], NT)


def body(img_feat, txt_feat, img_head, txt_head, logit_scale, logit_bias, pair_offset):
    rows, width = img_feat.shape
    dim = img_head.shape[1]
    blk, grp = lax.axis_index("blk"), lax.axis_index("grp")
    core, x, zh = blk % 2, blk // 4, (blk // 2) % 2
    zl, y = grp // 4, grp % 4
    idx = jnp.stack([core, jnp.where(core == 0, x, y), jnp.where(core == 0, y, x), zl]).astype(jnp.int32)
    m = 4 * rows

    h = 2 * rows
    off = pair_offset.reshape(1, rows)
    idx, off, img_feat, txt_feat = after(idx, off, img_feat, txt_feat)
    far = send(img_feat, across_z(1))
    near = [img_feat] + [send(img_feat, along(Y, -d)) for d in (1, 2, 3)]
    later, far, *near = after(txt_feat, far, *near)
    prev_pair = [send(later, along_blk(1)), send(later, across_z(2, along_blk(1)))]
    own_pair = [txt_feat, send(txt_feat, across_z(2))]
    distant = [far] + [send(far, along(Y, -d)) for d in (1, 2, 3)]
    *begun, wi, wt = call(
        lambda *r: first_kernel(rows, *r),
        [
            ((m, width), BF16),
            ((h, width), BF16),
            ((m, dim), F32),
            ((m, dim), BF16),
            ((m, 128), F32),
            ((h, dim), F32),
            ((h, dim), BF16),
            ((h, 128), F32),
            ((m, h), BF16),
            ((8, h), F32),
            ((width, dim), BF16),
            ((width, dim), BF16),
        ],
        2,
        9,
        [pltpu.VMEM((m, h), F32)],
        24,
    )(logit_scale, logit_bias, [near[0]], *near[1:], [own_pair[0]], own_pair[1], [img_head], [txt_head], [off])
    middle = call(
        lambda *r: second_kernel(rows, *r),
        [
            ((h, width), BF16),
            ((h, dim), F32),
            ((h, dim), BF16),
            ((h, 128), F32),
            ((m, h), BF16),
            ((8, h), F32),
        ],
        2,
        5,
        [pltpu.VMEM((m, h), F32)],
    )(logit_scale, logit_bias, begun[3], *prev_pair, wt, [off])

    pair, piece = ((2 * rows, dim), BF16), ((rows, dim), BF16)
    outs = call(
        lambda *r: main_kernel(rows, dim, *r),
        [pair] * 3 + [piece] * 2 + [((dim + 16, dim), F32), ((dim + 16, dim), BF16)] + [piece] * 4,
        3,
        21,
        [
            pltpu.VMEM((2 * m, width), BF16),
            pltpu.VMEM((m, width), BF16),
            pltpu.VMEM((m, dim), F32),
            pltpu.VMEM((2 * m, dim), BF16),
            pltpu.VMEM((m, dim), BF16),
            pltpu.VMEM((m, 128), F32),
            pltpu.VMEM((m, m), F32),
            pltpu.VMEM((2 * m, m), BF16),
            pltpu.VMEM((2 * m, dim), BF16),
            pltpu.VMEM((m, dim), BF16),
            pltpu.VMEM((8, m), F32),
        ],
        34,
    )(idx, logit_scale, logit_bias, *begun, wi, *middle, *distant)
    g0, g1, g3, g2a, g2b, keep, other, own_t, own_far, prev_t, prev_far = outs

    recv = send(other, along(CORE, 1))
    back = [send(prev_t, along_blk(-1)), send(prev_far, across_z(2, along_blk(-1)))]
    part, small, wide = dim // 4, dim // 16, dim // 128
    loss_block = ((16, 128), BF16)
    slots = pltpu.VMEM((4, 8, 128), F32)
    folded = ((small * wide + 16, 128), BF16)
    half = [((rows, dim), F32), ((rows, dim), BF16)]
    own1, a1, a2, a3, mark1 = call(
        lambda *r: core_sum_kernel(part, dim, *r),
        [((part, dim), F32)] + [((part * wide + 16, 128), BF16)] * 3 + [loss_block],
        1,
        2,
    )(idx, keep, recv)
    got = [send(a, by_core(X, Y, d)) for d, a in ((1, a1), (2, a2), (3, a3))]
    own2, b1, b2, b3, mark2 = call(
        lambda *r: stage_sum_kernel(part, small, dim, *r),
        [((small, dim), F32)] + [folded] * 3 + [loss_block],
        1,
        5,
        [pltpu.VMEM((part, dim), F32), slots],
    )(idx, own1, mark1, *got)
    got = [send(b, by_core(Y, X, d)) for d, b in ((1, b1), (2, b2), (3, b3))]
    *got, back[0], back[1] = after(*got, *back)
    (zpart,) = call(lambda *r: second_sum_kernel(small, dim, *r), [folded], 1, 5, [slots])(idx, own2, mark2, *got)
    zpart, g2a, g2b = after(zpart, g2a, g2b)
    got = [send(zpart, along(ZL, d)) for d in (1, 2, 3)]
    from_left, from_right = send(g2a, along(Y, 1)), send(g2b, along(Y, -1))
    (zline,) = call(
        lambda *r: line_sum_kernel(small, dim, *r), [folded], 1, 4, [pltpu.VMEM((4, small, dim), F32), slots]
    )(idx, zpart, *got)
    zline, from_left, from_right = after(zline, from_left, from_right)
    zrecv = send(zline, along(ZH, 1))
    to_right, to_left = call(lambda *r: relay_kernel(rows, *r), [pair] * 2, 0, 4)(g1, g3, from_left, from_right)
    left, right = send(to_right, along(Y, 1)), send(to_left, along(Y, -1))
    done, mark3 = call(
        lambda *r: pair_sum_kernel(small, dim, *r), [((small, dim), BF16), ((16, dim), BF16)], 0, 2
    )(zline, zrecv)
    done, own_far = after(done, own_far)
    got = [done] + [send(done, by_core(Y, X, d)) for d in (1, 2, 3)]
    own_in = send(own_far, across_z(2))
    *got, left, right = after(*got, left, right)
    img_own, img_out = call(lambda *r: image_sum_kernel(rows, *r), half, 0, 3)(g0, left, right)
    img_in = send(img_out, across_z(1))
    (quarter,) = call(lambda *r: quarter_kernel(small, *r), [((part, dim), BF16)], 1, 4)(idx, *got)
    got = [quarter] + [send(quarter, by_core(X, Y, d)) for d in (1, 2, 3)]
    (whole,) = call(lambda *r: whole_kernel(part, *r), [((dim + 16, dim), BF16)], 1, 5)(idx, *got, mark3)
    whole, img_in, own_in = after(whole, img_in, own_in)
    theirs = send(whole, along(CORE, 1))
    (txt_feat_grad,) = call(text_feat_kernel, [((rows, width), F32)], 0, 5, placed=False)(own_t, own_in, *back, wt)
    (img_feat_grad,) = call(feat_kernel, [((rows, width), F32)], 0, 3, placed=False)(img_own, img_in, wi)
    total_rows = rows * 256
    img_head_grad, txt_head_grad, loss = call(
        lambda *r: finish_kernel(dim, math.sqrt(total_rows), total_rows, *r),
        [((dim, dim), F32)] * 2 + [((1,), F32)],
        1,
        2,
        placed=False,
    )(idx, whole, theirs)

    return img_feat_grad, txt_feat_grad, img_head_grad, txt_head_grad, loss


def solution(mesh):
    rows = P(AXES, None)
    in_specs = (rows, rows, P(), P(), P(), P(), P(AXES))
    out_specs = (rows, rows, P(), P(), P())
    return jax.shard_map(body, mesh=mesh, in_specs=in_specs, out_specs=out_specs, check_vma=False)
```
